32 devices in a mesh: head: 4 (over x, core), blk: 8 (over z, y).
Axes of the slice: x: 2, y: 2, z: 4, core: 2. Of those that a mesh axis runs over, the one named last changes fastest.
Arguments:
- queries: bfloat16 [8, 512, 2048], P('blk', 'head'), may hold values from -10 to 10
- keys: bfloat16 [8, 512, 512], P('blk', 'head'), may hold values from -10 to 10
- values: bfloat16 [8, 512, 512], P('blk', 'head'), may hold values from -6 to 6
- position: int32 [8, 512], replicated, may hold values from 0 to 4095, as said below
- segment: int32 [8, 512], replicated, may hold values from 0 to 3, as said below
Outputs:
- attended: bfloat16 [8, 512, 2048], P('blk', 'head')
The draws below stay inside these ranges and needn't reach their ends.
Inputs may be any that keep to these rules, and one draw needn't show every extreme that they name: Each row b holds two runs of 256 consecutive positions in rising order, first c * 256 onward, then (15 - c) * 256 onward, with c a permutation of the rows; every position appears once. `segment`: documents are runs of consecutive positions; their numbers rise with position, start at 0 and may skip values.
All inputs are finite; a program needn't handle non-finite values.
Results may differ from the reference program's by a relative error of at most 0.007.
Values may be sent and summed in bfloat16 or wider, within the bound.
A program may use at most 128 MiB of HBM per device.

```python
import jax
import jax.numpy as jnp
from jax import lax

LOCAL_QUERY_HEADS = 16
LOCAL_KV_HEADS = 4
HEAD_SIZE = 128
TOKENS_PER_BLOCK = 512
STORED_BLOCKS = 8
SEQUENCE_TOKENS = 4096


def zig_layout(key):
    base = jax.random.fold_in(key, 200)
    order = jax.random.permutation(base, STORED_BLOCKS).astype(jnp.int32)
    half = TOKENS_PER_BLOCK // 2
    within = jnp.arange(half, dtype=jnp.int32)
    lower = order[:, None] * half + within[None, :]
    upper = (2 * STORED_BLOCKS - 1 - order)[:, None] * half + within[None, :]
    return jnp.concatenate([lower, upper], axis=1).astype(jnp.int32)


def draw_queries(key, part):
    key = jax.random.fold_in(key, 1)
    attention_result = jax.random.truncated_normal(key, -4.0, 4.0, (STORED_BLOCKS, TOKENS_PER_BLOCK, LOCAL_QUERY_HEADS, HEAD_SIZE), jnp.float32)
    return attention_result.reshape(STORED_BLOCKS, TOKENS_PER_BLOCK, LOCAL_QUERY_HEADS * HEAD_SIZE).astype(jnp.bfloat16)


def draw_keys(key, part):
    key = jax.random.fold_in(key, 2)
    attention_result = jax.random.truncated_normal(key, -4.0, 4.0, (STORED_BLOCKS, TOKENS_PER_BLOCK, LOCAL_KV_HEADS, HEAD_SIZE), jnp.float32)
    return attention_result.reshape(STORED_BLOCKS, TOKENS_PER_BLOCK, LOCAL_KV_HEADS * HEAD_SIZE).astype(jnp.bfloat16)


def draw_position(key, part):
    return zig_layout(key)


def draw_segment(key, part):
    placed = zig_layout(key)
    key = jax.random.fold_in(key, 7)
    bounds = jax.random.randint(key, (3,), 1, STORED_BLOCKS * TOKENS_PER_BLOCK).astype(jnp.int32)
    return jnp.sum((placed[:, :, None] >= bounds[None, None, :]).astype(jnp.int32), axis=-1).astype(jnp.int32)


def steps_of(key, extent, cuts, least, high):
    def one(axis_at, blocks):
        heights = jax.random.uniform(jax.random.fold_in(jax.random.fold_in(key, 6), axis_at), (blocks,), jnp.float32, least / len(cuts), high / len(cuts))
        return jnp.repeat(jnp.exp(heights), extent[axis_at] // blocks).reshape((-1,) + (1,) * (len(extent) - axis_at - 1))

    level = one(*cuts[0])
    for cut in cuts[1:]:
        level = level * one(*cut)
    return level


def scatter_about(stream_key, shape, spread, limit, cuts=(), kind=jnp.bfloat16):
    result = spread * jax.random.normal(stream_key, shape, jnp.float32)
    if cuts:
        result = result * steps_of(stream_key, shape, cuts, -0.22, 0.18)
    return jnp.clip(result, -limit, limit).astype(kind)


def setup_inputs(seed: int = 0) -> dict:
    key_list = jax.random.split(jax.random.key(seed), 6)
    return {
        "queries": draw_queries(jax.random.fold_in(key_list[5], 71), 0),
        "keys": draw_keys(jax.random.fold_in(key_list[5], 71), 0),
        "values": scatter_about(key_list[2], (STORED_BLOCKS, TOKENS_PER_BLOCK, LOCAL_KV_HEADS * HEAD_SIZE), 1.0, 6.0, ((0, 8), (1, 4))),
        "position": draw_position(jax.random.fold_in(key_list[5], 71), 0),
        "segment": draw_segment(jax.random.fold_in(key_list[5], 71), 0),
    }


masked_score = -1.0e30


def attend_block(block, gathered_keys, gathered_values, pos_all, seg_all):
    queries_blk, pos_blk, seg_blk = block
    visible = (seg_all[None, :] == seg_blk[:, None]) & (pos_all[None, :] <= pos_blk[:, None])
    query_group = LOCAL_QUERY_HEADS // LOCAL_KV_HEADS
    pieces = []
    for shared_kv_head in range(LOCAL_KV_HEADS):
        query_part = queries_blk[:, shared_kv_head * query_group:(shared_kv_head + 1) * query_group, :].astype(jnp.float32)
        key_part = gathered_keys[:, shared_kv_head, :].astype(jnp.float32)
        scores = jnp.einsum("tgd,sd->gts", query_part, key_part) * (HEAD_SIZE ** -0.5)
        scores = jnp.where(visible[None], scores, masked_score)
        row_top = jnp.max(scores, axis=-1, keepdims=True)
        weights = jnp.where(visible[None], jnp.exp(scores - row_top), 0.0)
        totals = jnp.sum(weights, axis=-1)
        rounded = lax.optimization_barrier(weights.astype(jnp.bfloat16)).astype(jnp.float32)
        context = jnp.einsum("gts,sd->tgd", rounded, gathered_values[:, shared_kv_head, :].astype(jnp.float32))
        pieces.append(context / jnp.transpose(totals)[:, :, None])
    joined = jnp.concatenate(pieces, axis=1)
    return joined.reshape(TOKENS_PER_BLOCK, LOCAL_QUERY_HEADS * HEAD_SIZE).astype(jnp.bfloat16)


def reference(queries, keys, values, position, segment):
    query_heads = queries.reshape(STORED_BLOCKS, TOKENS_PER_BLOCK, LOCAL_QUERY_HEADS, HEAD_SIZE)
    gathered_keys = keys.reshape(SEQUENCE_TOKENS, LOCAL_KV_HEADS, HEAD_SIZE)
    gathered_values = values.reshape(SEQUENCE_TOKENS, LOCAL_KV_HEADS, HEAD_SIZE)
    pos_all = position.reshape(SEQUENCE_TOKENS)
    seg_all = segment.reshape(SEQUENCE_TOKENS)

    def one_block(block):
        return attend_block(block, gathered_keys, gathered_values, pos_all, seg_all)

    return lax.map(one_block, (query_heads, position, segment))
```

```python
import functools
import math

import jax
import jax.numpy as jnp
from jax import lax
from jax.experimental import pallas as pl
from jax.experimental.pallas import tpu as pltpu
from jax.sharding import PartitionSpec as P

QUERY_HEADS = 16
KV_HEADS = 4
HEAD_SIZE = 128
MASKED = -1e30
SCALE = math.log2(math.e) / math.sqrt(HEAD_SIZE)
MESH = pl.DeviceIdType.MESH


def kernel(H, B, q_in, k_in, v_in, pos_ref, seg_ref, out_ref,
           qbuf, kv, segc, obuf, top, total, acc,
           first_send, q_recv, row_recv, sib_recv, fwd_send, sib_send, out_send, out_recv):
    Y = 2 * KV_HEADS // H
    Z = B // Y
    HQ = QUERY_HEADS // H
    HH = H // 2
    T = q_in.shape[0]
    R = qbuf.shape[1]
    width = HQ * HEAD_SIZE
    h = lax.axis_index("head")
    b = lax.axis_index("blk")
    chip, t = h // 2, h % 2
    z, y = b // Y, b % Y
    kv_head = chip * Y + y
    sibling = chip * 2 + 1 - t
    row_me = z * Y + t % Y

    barrier = pltpu.get_barrier_semaphore()
    for i in range(H):
        for r in range(Y):
            @pl.when(jnp.logical_or(h != i, y != r))
            def _():
                pl.semaphore_signal(barrier, inc=1, device_id={"head": i, "blk": z * Y + r}, device_id_type=MESH)

    @pl.when(z > 0)
    def _():
        pl.semaphore_signal(barrier, inc=1, device_id={"head": h, "blk": b - Y}, device_id_type=MESH)

    @pl.when(z < Z - 1)
    def _():
        pl.semaphore_signal(barrier, inc=1, device_id={"head": h, "blk": b + Y}, device_id_type=MESH)

    near = (z > 0).astype(jnp.int32) + (z < Z - 1).astype(jnp.int32)
    pl.semaphore_wait(barrier, H * Y - 1 + near)

    def part(i):
        return i // HH, pl.ds(pl.multiple_of((i % HH) * T, T), T)

    my_half, my_rows = part(h)

    def send(src, dst, send_sem, recv_sem, head, blk, may_be_me, wait=False):
        def remote():
            copy = pltpu.make_async_remote_copy(
                src_ref=src, dst_ref=dst, send_sem=send_sem, recv_sem=recv_sem,
                device_id={"head": head, "blk": blk}, device_id_type=MESH)
            copy.wait_send() if wait else copy.start()

        if not may_be_me:
            remote()
            return
        other = jnp.logical_or(head != h, blk != b)
        pl.when(other)(remote)
        if not wait:
            @pl.when(jnp.logical_not(other))
            def _():
                pltpu.make_async_copy(src, dst, recv_sem).start()

    def exchange(wait):
        for n, array in enumerate((k_in, v_in)):
            for d in range(KV_HEADS):
                d = (d + 1) % KV_HEADS
                k = (kv_head + d) % KV_HEADS
                cols = pl.ds(pl.multiple_of(k * HEAD_SIZE, HEAD_SIZE), HEAD_SIZE)
                send(array.at[:, cols], kv.at[n, b, my_half, my_rows, :],
                     first_send.at[n, d], row_recv.at[b],
                     (k // Y) * 2 + n, z * Y + k % Y, d == 0, wait)
        for half in range(2 // Y):
            for d in range(KV_HEADS):
                d = (d + 1) % KV_HEADS
                k = (kv_head + d) % KV_HEADS
                cols = pl.ds(pl.multiple_of((k * (2 // Y) + half) * width, width), width)
                core = half if Y == 1 else y
                send(q_in.at[:, cols], qbuf.at[my_half, my_rows, :],
                     first_send.at[2 + half, d], q_recv,
                     (k // Y) * 2 + core, z * Y + k % Y, d == 0, wait)

    exchange(False)

    def column(row, c):
        line = seg_ref[pl.ds(row, 1), :].astype(jnp.float32)
        segc[row] = jnp.transpose(jnp.broadcast_to(line, (HEAD_SIZE, 2 * R))).reshape(2, R, HEAD_SIZE)
        return c

    lax.fori_loop(0, B, column, 0)

    def wait_row(row):
        pltpu.make_async_copy(kv.at[t, row], kv.at[t, row], row_recv.at[row]).wait()

    def wait_sibling(row):
        pltpu.make_async_copy(kv.at[1 - t, row], kv.at[1 - t, row], sib_recv.at[row]).wait()

    def pass_on(row, wait=False):
        def copy(head, blk, send_sem, recv_sem):
            c = pltpu.make_async_remote_copy(
                src_ref=kv.at[t, row], dst_ref=kv.at[t, row], send_sem=send_sem, recv_sem=recv_sem,
                device_id={"head": head, "blk": blk}, device_id_type=MESH)
            c.wait_send() if wait else c.start()

        j = row // Y

        @pl.when(jnp.logical_and(j <= z, z < Z - 1))
        def _():
            copy(h, b + Y, fwd_send.at[0, row], row_recv.at[row])

        @pl.when(jnp.logical_and(j >= z, z > 0))
        def _():
            copy(h, b - Y, fwd_send.at[1, row], row_recv.at[row])

        copy(sibling, b, sib_send.at[row], sib_recv.at[row])

    def scores(g, q_half, keys, visible):
        q = qbuf[q_half, :, g * HEAD_SIZE:(g + 1) * HEAD_SIZE]
        s = lax.dot_general(keys, q, (((1,), (1,)), ((), ())), preferred_element_type=jnp.float32)
        return jnp.where(visible, s, MASKED)

    def seg_line(q_half):
        line = seg_ref[pl.ds(row_me, 1), :].astype(jnp.float32)
        return line[:, q_half * R:(q_half + 1) * R]

    def mask(col, line):
        return jnp.concatenate([col] * (R // HEAD_SIZE), axis=1) == line

    def update(g, which, q_half, keys, values_t, visible):
        s = scores(g, q_half, keys, visible)
        top_old = top[which, g]
        top_new = jnp.maximum(top_old, jnp.max(s, axis=0, keepdims=True))
        w = jnp.exp2((s - top_new) * SCALE)
        fade = jnp.exp2((top_old - top_new) * SCALE)
        tot = total[which, g] * fade + jnp.sum(w, axis=0, keepdims=True)
        a = acc[which, g] * fade + jnp.dot(values_t, w.astype(jnp.bfloat16), preferred_element_type=jnp.float32)
        return top_new, tot, a

    def own():
        rows = lax.broadcasted_iota(jnp.int32, (R, R), 0)
        columns = lax.broadcasted_iota(jnp.int32, (R, R), 1)
        for half in range(2):
            keys = kv[0, row_me, half]
            values_t = jnp.transpose(kv[1, row_me, half])
            visible = jnp.logical_and(mask(segc[row_me, half], seg_line(half)), rows <= columns)
            for g in range(HQ):
                s = scores(g, half, keys, visible)
                t_new = jnp.max(s, axis=0, keepdims=True)
                w = jnp.exp2((s - t_new) * SCALE)
                top[half, g] = t_new
                total[half, g] = jnp.sum(w, axis=0, keepdims=True)
                acc[half, g] = jnp.dot(values_t, w.astype(jnp.bfloat16), preferred_element_type=jnp.float32)
        keys = kv[0, row_me, 0]
        values_t = jnp.transpose(kv[1, row_me, 0])
        visible = mask(segc[row_me, 0], seg_line(1))
        for g in range(HQ):
            top[1, g], total[1, g], acc[1, g] = update(g, 1, 1, keys, values_t, visible)

    def attend(row):
        keys = kv[0, row, 0]
        values_t = jnp.transpose(kv[1, row, 0])
        col = segc[row, 0]
        visible = mask(col, seg_line(1))
        for g in range(HQ):
            top[1, g], total[1, g], acc[1, g] = update(g, 1, 1, keys, values_t, visible)
        which = (pos_ref[row, 0] > pos_ref[row_me, 0]).astype(jnp.int32)
        late = which == 1
        keys = jnp.where(late, kv[0, row, 1], keys)
        values_t = jnp.transpose(jnp.where(late, kv[1, row, 1], kv[1, row, 0]))
        visible = mask(jnp.where(late, segc[row, 1], col), jnp.where(late, seg_line(1), seg_line(0)))
        for g in range(HQ):
            new = update(g, which, which, keys, values_t, visible)
            for ref, value in zip((top, total, acc), new):
                ref[0, g] = jnp.where(late, ref[0, g], value)
                ref[1, g] = jnp.where(late, value, ref[1, g])

    for r in range(Y):
        wait_row(z * Y + r)
        pass_on(z * Y + r)
    pltpu.make_async_copy(qbuf, qbuf, q_recv).wait()
    for r in range(Y):
        wait_sibling(z * Y + r)
    own()
    for r in range(1, Y):
        attend(z * Y + (t + r) % Y)

    def step(u, c):
        s, r = 1 + u // Y, u % Y

        def side(way, do):
            j = z + s * (2 * way - 1)

            @pl.when(jnp.logical_and(j >= 0, j < Z))
            def _():
                do(j * Y + r)

        def arrive(row):
            wait_row(row)
            pass_on(row)

        def use(row):
            wait_sibling(row)
            attend(row)

        def each(way, c):
            side(way, use)
            return c

        side(0, arrive)
        side(1, arrive)
        lax.fori_loop(0, 2, each, 0)
        return c

    lax.fori_loop(0, (Z - 1) * Y, step, 0)

    slot = kv_head * (2 // Y) + (t if Y == 1 else 0)
    out_cols = pl.ds(pl.multiple_of(slot * width, width), width)

    def send_out(half, wait):
        for e in range(HH):
            e = (e + 1) % HH
            i = half * HH + (h + e) % HH
            i_half, i_rows = part(i)
            send(obuf.at[i_half, i_rows, :], out_ref.at[:, out_cols],
                 out_send.at[half, e], out_recv, i, row_me, True, wait)

    for half in range(2):
        for g in range(HQ):
            o = acc[half, g] / total[half, g]
            obuf[half, :, g * HEAD_SIZE:(g + 1) * HEAD_SIZE] = jnp.transpose(o).astype(jnp.bfloat16)
        send_out(half, False)

    exchange(True)

    def drain(row, c):
        pass_on(row, True)
        return c

    lax.fori_loop(0, B, drain, 0)
    for half in range(2):
        send_out(half, True)
    pltpu.make_async_copy(out_ref, out_ref, out_recv).wait()


def local(queries, keys, values, position, segment):
    H, B = lax.axis_size("head"), lax.axis_size("blk")
    T = queries.shape[1]
    Y = 2 * KV_HEADS // H
    HQ = QUERY_HEADS // H
    R = position.shape[1] // 2
    pairs = B * (2 * R) ** 2 * HQ * 17 // 32
    out = pl.pallas_call(
        functools.partial(kernel, H, B),
        out_shape=jax.ShapeDtypeStruct((T, QUERY_HEADS * HEAD_SIZE), jnp.bfloat16),
        in_specs=[pl.BlockSpec(memory_space=pl.ANY)] * 3
        + [pl.BlockSpec(memory_space=pltpu.SMEM), pl.BlockSpec(memory_space=pltpu.VMEM)],
        out_specs=pl.BlockSpec(memory_space=pltpu.VMEM),
        scratch_shapes=[
            pltpu.VMEM((2, R, HQ * HEAD_SIZE), jnp.bfloat16),
            pltpu.VMEM((2, B, 2, R, HEAD_SIZE), jnp.bfloat16),
            pltpu.VMEM((B, 2, R, HEAD_SIZE), jnp.float32),
            pltpu.VMEM((2, R, HQ * HEAD_SIZE), jnp.bfloat16),
            pltpu.VMEM((2, HQ, 1, R), jnp.float32),
            pltpu.VMEM((2, HQ, 1, R), jnp.float32),
            pltpu.VMEM((2, HQ, HEAD_SIZE, R), jnp.float32),
            pltpu.SemaphoreType.DMA((2 + 2 // Y, KV_HEADS)),
            pltpu.SemaphoreType.DMA,
            pltpu.SemaphoreType.DMA((B,)),
            pltpu.SemaphoreType.DMA((B,)),
            pltpu.SemaphoreType.DMA((2, B)),
            pltpu.SemaphoreType.DMA((B,)),
            pltpu.SemaphoreType.DMA((2, H // 2)),
            pltpu.SemaphoreType.DMA,
        ],
        compiler_params=pltpu.CompilerParams(
            collective_id=0, has_side_effects=True, vmem_limit_bytes=40 * 2**20
        ),
        cost_estimate=pl.CostEstimate(
            flops=4 * pairs * HEAD_SIZE, bytes_accessed=8 * T * QUERY_HEADS * HEAD_SIZE, transcendentals=pairs
        ),
    )(queries[0], keys[0], values[0], position, segment)
    return out[None]


def solution(mesh):
    return jax.shard_map(
        local,
        mesh=mesh,
        in_specs=(P("blk", "head", None), P("blk", "head", None), P("blk", "head", None), P(), P()),
        out_specs=P("blk", "head", None),
        check_vma=False,
    )
```

```python
import functools
import math

import jax
import jax.numpy as jnp
from jax import lax
from jax.experimental import pallas as pl
from jax.experimental.pallas import tpu as pltpu
from jax.sharding import PartitionSpec as P

QUERY_HEADS = 16
KV_HEADS = 4
HEAD_SIZE = 128
MASKED = -1e30
SCALE = math.log2(math.e) / math.sqrt(HEAD_SIZE)
MESH = pl.DeviceIdType.MESH


def kernel(H, B, q_in, k_in, v_in, pos_ref, seg_ref, out_ref,
           qbuf, kv, segc, obuf, top, total, acc, bias, pos_buf, seg_buf, small,
           first_send, q_recv, row_recv, sib_recv, fwd_send, sib_send, out_send, out_recv):
    Y = 2 * KV_HEADS // H
    Z = B // Y
    HQ = QUERY_HEADS // H
    HH = H // 2
    T = q_in.shape[0]
    R = qbuf.shape[1]
    width = HQ * HEAD_SIZE
    h = lax.axis_index("head")
    b = lax.axis_index("blk")
    chip, t = h // 2, h % 2
    z, y = b // Y, b % Y
    kv_head = chip * Y + y
    sibling = chip * 2 + 1 - t
    row_me = z * Y + t % Y

    fetch = [pltpu.make_async_copy(pos_ref, pos_buf, small.at[0]), pltpu.make_async_copy(seg_ref, seg_buf, small.at[1])]
    for copy in fetch:
        copy.start()

    barrier = pltpu.get_barrier_semaphore()
    for i in range(H):
        for r in range(Y):
            @pl.when(jnp.logical_or(h != i, y != r))
            def _():
                pl.semaphore_signal(barrier, inc=1, device_id={"head": i, "blk": z * Y + r}, device_id_type=MESH)

    @pl.when(z > 0)
    def _():
        pl.semaphore_signal(barrier, inc=1, device_id={"head": h, "blk": b - Y}, device_id_type=MESH)

    @pl.when(z < Z - 1)
    def _():
        pl.semaphore_signal(barrier, inc=1, device_id={"head": h, "blk": b + Y}, device_id_type=MESH)

    near = (z > 0).astype(jnp.int32) + (z < Z - 1).astype(jnp.int32)
    pl.semaphore_wait(barrier, H * Y - 1 + near)

    def part(i):
        return i // HH, pl.ds(pl.multiple_of((i % HH) * T, T), T)

    my_half, my_rows = part(h)

    def send(src, dst, send_sem, recv_sem, head, blk, may_be_me, wait=False):
        def remote():
            copy = pltpu.make_async_remote_copy(
                src_ref=src, dst_ref=dst, send_sem=send_sem, recv_sem=recv_sem,
                device_id={"head": head, "blk": blk}, device_id_type=MESH)
            copy.wait_send() if wait else copy.start()

        if not may_be_me:
            remote()
            return
        other = jnp.logical_or(head != h, blk != b)
        pl.when(other)(remote)
        if not wait:
            @pl.when(jnp.logical_not(other))
            def _():
                pltpu.make_async_copy(src, dst, recv_sem).start()

    def exchange(wait):
        for n, array in enumerate((k_in, v_in)):
            for d in range(KV_HEADS):
                d = (d + 1) % KV_HEADS
                k = (kv_head + d) % KV_HEADS
                cols = pl.ds(pl.multiple_of(k * HEAD_SIZE, HEAD_SIZE), HEAD_SIZE)
                send(array.at[:, cols], kv.at[n, b, my_half, my_rows, :],
                     first_send.at[n, d], row_recv.at[b],
                     (k // Y) * 2 + n, z * Y + k % Y, d == 0, wait)
        for half in range(2 // Y):
            for d in range(KV_HEADS):
                d = (d + 1) % KV_HEADS
                k = (kv_head + d) % KV_HEADS
                cols = pl.ds(pl.multiple_of((k * (2 // Y) + half) * width, width), width)
                core = half if Y == 1 else y
                send(q_in.at[:, cols], qbuf.at[my_half, my_rows, :],
                     first_send.at[2 + half, d], q_recv,
                     (k // Y) * 2 + core, z * Y + k % Y, d == 0, wait)

    exchange(False)
    for copy in fetch:
        copy.wait()

    def column(row, c):
        line = seg_buf[pl.ds(row, 1), :].astype(jnp.float32)
        segc[row] = jnp.transpose(jnp.broadcast_to(line, (HEAD_SIZE, 2 * R))).reshape(2, R, HEAD_SIZE)
        return c

    lax.fori_loop(0, B, column, 0)

    def wait_row(row):
        pltpu.make_async_copy(kv.at[t, row], kv.at[t, row], row_recv.at[row]).wait()

    def wait_sibling(row):
        pltpu.make_async_copy(kv.at[1 - t, row], kv.at[1 - t, row], sib_recv.at[row]).wait()

    def pass_on(row, wait=False):
        def copy(head, blk, send_sem, recv_sem):
            c = pltpu.make_async_remote_copy(
                src_ref=kv.at[t, row], dst_ref=kv.at[t, row], send_sem=send_sem, recv_sem=recv_sem,
                device_id={"head": head, "blk": blk}, device_id_type=MESH)
            c.wait_send() if wait else c.start()

        j = row // Y

        @pl.when(jnp.logical_and(j <= z, z < Z - 1))
        def _():
            copy(h, b + Y, fwd_send.at[0, row], row_recv.at[row])

        @pl.when(jnp.logical_and(j >= z, z > 0))
        def _():
            copy(h, b - Y, fwd_send.at[1, row], row_recv.at[row])

        copy(sibling, b, sib_send.at[row], sib_recv.at[row])

    def seg_line(q_half):
        line = seg_buf[pl.ds(row_me, 1), :].astype(jnp.float32)
        return line[:, q_half * R:(q_half + 1) * R]

    def hide(n, col, line, extra=None):
        visible = jnp.concatenate([col] * (R // HEAD_SIZE), axis=1) == line
        if extra is not None:
            visible = jnp.logical_and(visible, extra)
        bias[n] = jnp.where(visible, 0.0, MASKED)

    def tile(g, n, q_half, keys, values_t):
        q = qbuf[q_half, :, g * HEAD_SIZE:(g + 1) * HEAD_SIZE]
        s = lax.dot_general(keys, q, (((1,), (1,)), ((), ())), preferred_element_type=jnp.float32)
        s = s + bias[n]
        m = jnp.max(s, axis=0, keepdims=True)
        w = jnp.exp2((s - m) * SCALE)
        return (m, jnp.sum(w, axis=0, keepdims=True),
                jnp.dot(values_t, w.astype(jnp.bfloat16), preferred_element_type=jnp.float32))

    def merge(*states):
        m = functools.reduce(jnp.maximum, [x[0] for x in states])
        fades = [jnp.exp2((x[0] - m) * SCALE) for x in states]
        return (m, sum(x[1] * f for x, f in zip(states, fades)),
                sum(x[2] * f for x, f in zip(states, fades)))

    def load(which, g):
        return top[which, g], total[which, g], acc[which, g]

    def store(which, g, state):
        top[which, g], total[which, g], acc[which, g] = state

    def own():
        rows = lax.broadcasted_iota(jnp.int32, (R, R), 0)
        columns = lax.broadcasted_iota(jnp.int32, (R, R), 1)
        keys = [kv[0, row_me, half] for half in range(2)]
        values_t = [jnp.transpose(kv[1, row_me, half]) for half in range(2)]
        for half in range(2):
            hide(half, segc[row_me, half], seg_line(half), rows <= columns)
        hide(2, segc[row_me, 0], seg_line(1))
        for g in range(HQ):
            store(0, g, tile(g, 0, 0, keys[0], values_t[0]))
            store(1, g, merge(tile(g, 1, 1, keys[1], values_t[1]), tile(g, 2, 1, keys[0], values_t[0])))

    def attend(row):
        which = (pos_buf[row, 0] > pos_buf[row_me, 0]).astype(jnp.int32)
        late = which == 1
        keys = kv[0, row, 0]
        values_t = jnp.transpose(kv[1, row, 0])
        col = segc[row, 0]
        hide(0, col, seg_line(1))
        keys_b = jnp.where(late, kv[0, row, 1], keys)
        values_b = jnp.transpose(jnp.where(late, kv[1, row, 1], kv[1, row, 0]))
        hide(1, jnp.where(late, segc[row, 1], col), jnp.where(late, seg_line(1), seg_line(0)))
        for g in range(HQ):
            one = tile(g, 0, 1, keys, values_t)
            m, tot, a = tile(g, 1, which, keys_b, values_b)
            store(1, g, merge(load(1, g), one, (jnp.where(late, m, MASKED), tot, a)))
            store(0, g, merge(load(0, g), (jnp.where(late, MASKED, m), tot, a)))

    for r in range(Y):
        wait_row(z * Y + r)
        pass_on(z * Y + r)
    pltpu.make_async_copy(qbuf, qbuf, q_recv).wait()
    for r in range(Y):
        wait_sibling(z * Y + r)
    own()
    for r in range(1, Y):
        attend(z * Y + (t + r) % Y)

    def step(u, c):
        s, r = 1 + u // Y, u % Y

        def side(way, do):
            j = z + s * (2 * way - 1)

            @pl.when(jnp.logical_and(j >= 0, j < Z))
            def _():
                do(j * Y + r)

        def arrive(row):
            wait_row(row)
            pass_on(row)

        def use(row):
            wait_sibling(row)
            attend(row)

        def each(way, c):
            side(way, use)
            return c

        side(0, arrive)
        side(1, arrive)
        lax.fori_loop(0, 2, each, 0)
        return c

    lax.fori_loop(0, (Z - 1) * Y, step, 0)

    slot = kv_head * (2 // Y) + (t if Y == 1 else 0)
    out_cols = pl.ds(pl.multiple_of(slot * width, width), width)

    def send_out(half, wait):
        for e in range(HH):
            e = (e + 1) % HH
            i = half * HH + (h + e) % HH
            i_half, i_rows = part(i)
            send(obuf.at[i_half, i_rows, :], out_ref.at[:, out_cols],
                 out_send.at[half, e], out_recv, i, row_me, True, wait)

    for half in range(2):
        for g in range(HQ):
            o = acc[half, g] / total[half, g]
            obuf[half, :, g * HEAD_SIZE:(g + 1) * HEAD_SIZE] = jnp.transpose(o).astype(jnp.bfloat16)
        send_out(half, False)

    exchange(True)

    def drain(row, c):
        pass_on(row, True)
        return c

    lax.fori_loop(0, B, drain, 0)
    for half in range(2):
        send_out(half, True)
    pltpu.make_async_copy(out_ref, out_ref, out_recv).wait()


def local(queries, keys, values, position, segment):
    H, B = lax.axis_size("head"), lax.axis_size("blk")
    T = queries.shape[1]
    Y = 2 * KV_HEADS // H
    HQ = QUERY_HEADS // H
    R = position.shape[1] // 2
    pairs = B * (2 * R) ** 2 * HQ * 17 // 32
    out = pl.pallas_call(
        functools.partial(kernel, H, B),
        out_shape=jax.ShapeDtypeStruct((T, QUERY_HEADS * HEAD_SIZE), jnp.bfloat16),
        in_specs=[pl.BlockSpec(memory_space=pltpu.HBM)] * 5,
        out_specs=pl.BlockSpec(memory_space=pl.ANY),
        scratch_shapes=[
            pltpu.VMEM((2, R, HQ * HEAD_SIZE), jnp.bfloat16),
            pltpu.VMEM((2, B, 2, R, HEAD_SIZE), jnp.bfloat16),
            pltpu.VMEM((B, 2, R, HEAD_SIZE), jnp.float32),
            pltpu.VMEM((2, R, HQ * HEAD_SIZE), jnp.bfloat16),
            pltpu.VMEM((2, HQ, 1, R), jnp.float32),
            pltpu.VMEM((2, HQ, 1, R), jnp.float32),
            pltpu.VMEM((2, HQ, HEAD_SIZE, R), jnp.float32),
            pltpu.VMEM((3, R, R), jnp.float32),
            pltpu.SMEM(position.shape, jnp.int32),
            pltpu.VMEM(segment.shape, jnp.int32),
            pltpu.SemaphoreType.DMA((2,)),
            pltpu.SemaphoreType.DMA((2 + 2 // Y, KV_HEADS)),
            pltpu.SemaphoreType.DMA,
            pltpu.SemaphoreType.DMA((B,)),
            pltpu.SemaphoreType.DMA((B,)),
            pltpu.SemaphoreType.DMA((2, B)),
            pltpu.SemaphoreType.DMA((B,)),
            pltpu.SemaphoreType.DMA((2, H // 2)),
            pltpu.SemaphoreType.DMA,
        ],
        compiler_params=pltpu.CompilerParams(
            collective_id=0, has_side_effects=True, vmem_limit_bytes=60 * 2**20
        ),
        cost_estimate=pl.CostEstimate(
            flops=4 * pairs * HEAD_SIZE, bytes_accessed=8 * T * QUERY_HEADS * HEAD_SIZE, transcendentals=pairs
        ),
    )(queries[0], keys[0], values[0], position, segment)
    return out[None]


def solution(mesh):
    return jax.shard_map(
        local,
        mesh=mesh,
        in_specs=(P("blk", "head", None), P("blk", "head", None), P("blk", "head", None), P(), P()),
        out_specs=P("blk", "head", None),
        check_vma=False,
    )
```

```python
import functools
import math

import jax
import jax.numpy as jnp
from jax import lax
from jax.experimental import pallas as pl
from jax.experimental.pallas import tpu as pltpu
from jax.sharding import PartitionSpec as P

QUERY_HEADS = 16
KV_HEADS = 4
HEAD_SIZE = 128
MASKED = -1e30
SCALE = math.log2(math.e) / math.sqrt(HEAD_SIZE)
MESH = pl.DeviceIdType.MESH


def kernel(H, B, q_in, k_in, v_in, pos_ref, seg_ref, out_ref,
           qbuf, kv, segc, obuf, top, total, acc, bias, pos_buf, seg_buf, small,
           first_send, q_recv, row_recv, sib_recv, fwd_send, sib_send, out_send, out_recv):
    Y = 2 * KV_HEADS // H
    Z = B // Y
    HQ = QUERY_HEADS // H
    HH = H // 2
    T = q_in.shape[0]
    R = qbuf.shape[1]
    width = HQ * HEAD_SIZE
    h = lax.axis_index("head")
    b = lax.axis_index("blk")
    chip, t = h // 2, h % 2
    z, y = b // Y, b % Y
    kv_head = chip * Y + y
    sibling = chip * 2 + 1 - t
    row_me = z * Y + t % Y

    fetch = [pltpu.make_async_copy(pos_ref, pos_buf, small.at[0]), pltpu.make_async_copy(seg_ref, seg_buf, small.at[1])]
    for copy in fetch:
        copy.start()

    barrier = pltpu.get_barrier_semaphore()
    for i in range(H):
        for r in range(Y):
            @pl.when(jnp.logical_or(h != i, y != r))
            def _():
                pl.semaphore_signal(barrier, inc=1, device_id={"head": i, "blk": z * Y + r}, device_id_type=MESH)

    @pl.when(z > 0)
    def _():
        pl.semaphore_signal(barrier, inc=1, device_id={"head": h, "blk": b - Y}, device_id_type=MESH)

    @pl.when(z < Z - 1)
    def _():
        pl.semaphore_signal(barrier, inc=1, device_id={"head": h, "blk": b + Y}, device_id_type=MESH)

    near = (z > 0).astype(jnp.int32) + (z < Z - 1).astype(jnp.int32)
    pl.semaphore_wait(barrier, H * Y - 1 + near)

    def part(i):
        return i // HH, pl.ds(pl.multiple_of((i % HH) * T, T), T)

    my_half, my_rows = part(h)

    def send(src, dst, send_sem, recv_sem, head, blk, may_be_me, wait=False):
        def remote():
            copy = pltpu.make_async_remote_copy(
                src_ref=src, dst_ref=dst, send_sem=send_sem, recv_sem=recv_sem,
                device_id={"head": head, "blk": blk}, device_id_type=MESH)
            copy.wait_send() if wait else copy.start()

        if not may_be_me:
            remote()
            return
        other = jnp.logical_or(head != h, blk != b)
        pl.when(other)(remote)
        if not wait:
            @pl.when(jnp.logical_not(other))
            def _():
                pltpu.make_async_copy(src, dst, recv_sem).start()

    def exchange_kv(wait):
        for n, array in enumerate((k_in, v_in)):
            for d in range(KV_HEADS):
                d = (d + 1) % KV_HEADS
                k = (kv_head + d) % KV_HEADS
                cols = pl.ds(pl.multiple_of(k * HEAD_SIZE, HEAD_SIZE), HEAD_SIZE)
                send(array.at[:, cols], kv.at[n, b, my_half, my_rows, :],
                     first_send.at[n, d], row_recv.at[b],
                     (k // Y) * 2 + n, z * Y + k % Y, d == 0, wait)

    def exchange_q(wait):
        for half in range(2 // Y):
            for d in range(KV_HEADS):
                d = (d + 1) % KV_HEADS
                k = (kv_head + d) % KV_HEADS
                cols = pl.ds(pl.multiple_of((k * (2 // Y) + half) * width, width), width)
                core = half if Y == 1 else y
                send(q_in.at[:, cols], qbuf.at[my_half, my_rows, :],
                     first_send.at[2 + half, d], q_recv,
                     (k // Y) * 2 + core, z * Y + k % Y, d == 0, wait)

    def wait_row(row):
        pltpu.make_async_copy(kv.at[t, row], kv.at[t, row], row_recv.at[row]).wait()

    def wait_sibling(row):
        pltpu.make_async_copy(kv.at[1 - t, row], kv.at[1 - t, row], sib_recv.at[row]).wait()

    def pass_on(row, wait=False):
        def copy(head, blk, send_sem, recv_sem):
            c = pltpu.make_async_remote_copy(
                src_ref=kv.at[t, row], dst_ref=kv.at[t, row], send_sem=send_sem, recv_sem=recv_sem,
                device_id={"head": head, "blk": blk}, device_id_type=MESH)
            c.wait_send() if wait else c.start()

        j = row // Y

        @pl.when(jnp.logical_and(j <= z, z < Z - 1))
        def _():
            copy(h, b + Y, fwd_send.at[0, row], row_recv.at[row])

        @pl.when(jnp.logical_and(j >= z, z > 0))
        def _():
            copy(h, b - Y, fwd_send.at[1, row], row_recv.at[row])

        copy(sibling, b, sib_send.at[row], sib_recv.at[row])

    def seg_line(q_half):
        line = seg_buf[pl.ds(row_me, 1), :].astype(jnp.float32)
        return line[:, q_half * R:(q_half + 1) * R]

    def hide(n, col, line, extra=None):
        visible = jnp.concatenate([col] * (R // HEAD_SIZE), axis=1) == line
        if extra is not None:
            visible = jnp.logical_and(visible, extra)
        bias[n] = jnp.where(visible, 0.0, MASKED)

    def tile(g, n, q_half, keys, values_t):
        q = qbuf[q_half, :, g * HEAD_SIZE:(g + 1) * HEAD_SIZE]
        s = lax.dot_general(keys, q, (((1,), (1,)), ((), ())), preferred_element_type=jnp.float32)
        s = s + bias[n]
        m = jnp.max(s, axis=0, keepdims=True)
        w = jnp.exp2((s - m) * SCALE)
        return (m, jnp.sum(w, axis=0, keepdims=True),
                jnp.dot(values_t, w.astype(jnp.bfloat16), preferred_element_type=jnp.float32))

    def merge(*states):
        m = functools.reduce(jnp.maximum, [x[0] for x in states])
        fades = [jnp.exp2((x[0] - m) * SCALE) for x in states]
        return (m, sum(x[1] * f for x, f in zip(states, fades)),
                sum(x[2] * f for x, f in zip(states, fades)))

    def load(which, g):
        return top[which, g], total[which, g], acc[which, g]

    def store(which, g, state):
        top[which, g], total[which, g], acc[which, g] = state

    def own():
        rows = lax.broadcasted_iota(jnp.int32, (R, R), 0)
        columns = lax.broadcasted_iota(jnp.int32, (R, R), 1)
        keys = [kv[0, row_me, half] for half in range(2)]
        values_t = [jnp.transpose(kv[1, row_me, half]) for half in range(2)]
        for half in range(2):
            hide(half, segc[row_me, half], seg_line(half), rows <= columns)
        hide(2, segc[row_me, 0], seg_line(1))
        for g in range(HQ):
            store(0, g, tile(g, 0, 0, keys[0], values_t[0]))
            store(1, g, merge(tile(g, 1, 1, keys[1], values_t[1]), tile(g, 2, 1, keys[0], values_t[0])))

    def attend(row):
        which = (pos_buf[row, 0] > pos_buf[row_me, 0]).astype(jnp.int32)
        late = which == 1
        keys = kv[0, row, 0]
        values_t = jnp.transpose(kv[1, row, 0])
        col = segc[row, 0]
        hide(0, col, seg_line(1))
        keys_b = jnp.where(late, kv[0, row, 1], keys)
        values_b = jnp.transpose(jnp.where(late, kv[1, row, 1], kv[1, row, 0]))
        hide(1, jnp.where(late, segc[row, 1], col), jnp.where(late, seg_line(1), seg_line(0)))
        for g in range(HQ):
            one = tile(g, 0, 1, keys, values_t)
            m, tot, a = tile(g, 1, which, keys_b, values_b)
            store(1, g, merge(load(1, g), one, (jnp.where(late, m, MASKED), tot, a)))
            store(0, g, merge(load(0, g), (jnp.where(late, MASKED, m), tot, a)))

    def side(u, way, do):
        j = z + (1 + u // Y) * (2 * way - 1)

        @pl.when(jnp.logical_and(j >= 0, j < Z))
        def _():
            do(j * Y + u % Y)

    def arrive_row(row):
        wait_row(row)
        pass_on(row)

    def use_row(row):
        wait_sibling(row)
        attend(row)

    def arrive(u):
        side(u, 0, arrive_row)
        side(u, 1, arrive_row)

    exchange_kv(False)
    for copy in fetch:
        copy.wait()
    for r in range(Y):
        wait_row(z * Y + r)
        pass_on(z * Y + r)
    exchange_q(False)

    def column(row, c):
        line = seg_buf[pl.ds(row, 1), :].astype(jnp.float32)
        segc[row] = jnp.transpose(jnp.broadcast_to(line, (HEAD_SIZE, 2 * R))).reshape(2, R, HEAD_SIZE)
        return c

    lax.fori_loop(0, B, column, 0)

    units = (Z - 1) * Y
    between = jnp.logical_and(z > 0, z < Z - 1)
    ahead = jnp.where(between, 4, 2)
    for u in range(min(2, units)):
        arrive(u)
    pltpu.make_async_copy(qbuf, qbuf, q_recv).wait()
    for r in range(Y):
        wait_sibling(z * Y + r)
    own()

    def early(u):
        @pl.when(jnp.logical_and(between, u < units))
        def _():
            arrive(u)

    early(2)
    for r in range(1, Y):
        attend(z * Y + (t + r) % Y)
    early(3)

    def step(u, c):
        def each(way, c):
            side(u, way, use_row)
            return c

        lax.fori_loop(0, 2, each, 0)

        @pl.when(u + ahead < units)
        def _():
            arrive(u + ahead)

        return c

    lax.fori_loop(0, units, step, 0)

    slot = kv_head * (2 // Y) + (t if Y == 1 else 0)
    out_cols = pl.ds(pl.multiple_of(slot * width, width), width)

    def send_out(half, wait):
        for e in range(HH):
            e = (e + 1) % HH
            i = half * HH + (h + e) % HH
            i_half, i_rows = part(i)
            send(obuf.at[i_half, i_rows, :], out_ref.at[:, out_cols],
                 out_send.at[half, e], out_recv, i, row_me, True, wait)

    for half in range(2):
        for g in range(HQ):
            o = acc[half, g] / total[half, g]
            obuf[half, :, g * HEAD_SIZE:(g + 1) * HEAD_SIZE] = jnp.transpose(o).astype(jnp.bfloat16)
        send_out(half, False)

    exchange_kv(True)
    exchange_q(True)

    def drain(row, c):
        pass_on(row, True)
        return c

    lax.fori_loop(0, B, drain, 0)
    for half in range(2):
        send_out(half, True)
    pltpu.make_async_copy(out_ref, out_ref, out_recv).wait()


def local(queries, keys, values, position, segment):
    H, B = lax.axis_size("head"), lax.axis_size("blk")
    T = queries.shape[1]
    Y = 2 * KV_HEADS // H
    HQ = QUERY_HEADS // H
    R = position.shape[1] // 2
    pairs = B * (2 * R) ** 2 * HQ * 17 // 32
    out = pl.pallas_call(
        functools.partial(kernel, H, B),
        out_shape=jax.ShapeDtypeStruct((T, QUERY_HEADS * HEAD_SIZE), jnp.bfloat16),
        in_specs=[pl.BlockSpec(memory_space=pltpu.HBM)] * 5,
        out_specs=pl.BlockSpec(memory_space=pl.ANY),
        scratch_shapes=[
            pltpu.VMEM((2, R, HQ * HEAD_SIZE), jnp.bfloat16),
            pltpu.VMEM((2, B, 2, R, HEAD_SIZE), jnp.bfloat16),
            pltpu.VMEM((B, 2, R, HEAD_SIZE), jnp.float32),
            pltpu.VMEM((2, R, HQ * HEAD_SIZE), jnp.bfloat16),
            pltpu.VMEM((2, HQ, 1, R), jnp.float32),
            pltpu.VMEM((2, HQ, 1, R), jnp.float32),
            pltpu.VMEM((2, HQ, HEAD_SIZE, R), jnp.float32),
            pltpu.VMEM((3, R, R), jnp.float32),
            pltpu.SMEM(position.shape, jnp.int32),
            pltpu.VMEM(segment.shape, jnp.int32),
            pltpu.SemaphoreType.DMA((2,)),
            pltpu.SemaphoreType.DMA((2 + 2 // Y, KV_HEADS)),
            pltpu.SemaphoreType.DMA,
            pltpu.SemaphoreType.DMA((B,)),
            pltpu.SemaphoreType.DMA((B,)),
            pltpu.SemaphoreType.DMA((2, B)),
            pltpu.SemaphoreType.DMA((B,)),
            pltpu.SemaphoreType.DMA((2, H // 2)),
            pltpu.SemaphoreType.DMA,
        ],
        compiler_params=pltpu.CompilerParams(
            collective_id=0, has_side_effects=True, vmem_limit_bytes=60 * 2**20
        ),
        cost_estimate=pl.CostEstimate(
            flops=4 * pairs * HEAD_SIZE, bytes_accessed=8 * T * QUERY_HEADS * HEAD_SIZE, transcendentals=pairs
        ),
    )(queries[0], keys[0], values[0], position, segment)
    return out[None]


def solution(mesh):
    return jax.shard_map(
        local,
        mesh=mesh,
        in_specs=(P("blk", "head", None), P("blk", "head", None), P("blk", "head", None), P(), P()),
        out_specs=P("blk", "head", None),
        check_vma=False,
    )
```

```python
import functools
import math

import jax
import jax.numpy as jnp
from jax import lax
from jax.experimental import pallas as pl
from jax.experimental.pallas import tpu as pltpu
from jax.sharding import PartitionSpec as P

QUERY_HEADS = 16
KV_HEADS = 4
HEAD_SIZE = 128
MASKED = -1e30
SCALE = math.log2(math.e) / math.sqrt(HEAD_SIZE)
MESH = pl.DeviceIdType.MESH


def kernel(H, B, q_in, k_in, v_in, pos_ref, seg_ref, out_ref,
           qbuf, kv, segc, obuf, top, total, acc, qt, pos_buf, seg_buf, small,
           first_send, q_recv, row_recv, sib_recv, fwd_send, sib_send, out_send, out_recv):
    Y = 2 * KV_HEADS // H
    Z = B // Y
    HQ = QUERY_HEADS // H
    HH = H // 2
    T = q_in.shape[0]
    R = qbuf.shape[1]
    width = HQ * HEAD_SIZE
    h = lax.axis_index("head")
    b = lax.axis_index("blk")
    chip, t = h // 2, h % 2
    z, y = b // Y, b % Y
    kv_head = chip * Y + y
    sibling = chip * 2 + 1 - t
    row_me = z * Y + t % Y

    fetch = [pltpu.make_async_copy(pos_ref, pos_buf, small.at[0]), pltpu.make_async_copy(seg_ref, seg_buf, small.at[1])]
    for copy in fetch:
        copy.start()

    barrier = pltpu.get_barrier_semaphore()
    for i in range(H):
        for r in range(Y):
            @pl.when(jnp.logical_or(h != i, y != r))
            def _():
                pl.semaphore_signal(barrier, inc=1, device_id={"head": i, "blk": z * Y + r}, device_id_type=MESH)

    @pl.when(z > 0)
    def _():
        pl.semaphore_signal(barrier, inc=1, device_id={"head": h, "blk": b - Y}, device_id_type=MESH)

    @pl.when(z < Z - 1)
    def _():
        pl.semaphore_signal(barrier, inc=1, device_id={"head": h, "blk": b + Y}, device_id_type=MESH)

    near = (z > 0).astype(jnp.int32) + (z < Z - 1).astype(jnp.int32)
    pl.semaphore_wait(barrier, H * Y - 1 + near)

    def part(i):
        return i // HH, pl.ds(pl.multiple_of((i % HH) * T, T), T)

    my_half, my_rows = part(h)

    def send(src, dst, send_sem, recv_sem, head, blk, may_be_me, wait=False):
        def remote():
            copy = pltpu.make_async_remote_copy(
                src_ref=src, dst_ref=dst, send_sem=send_sem, recv_sem=recv_sem,
                device_id={"head": head, "blk": blk}, device_id_type=MESH)
            copy.wait_send() if wait else copy.start()

        if not may_be_me:
            remote()
            return
        other = jnp.logical_or(head != h, blk != b)
        pl.when(other)(remote)
        if not wait:
            @pl.when(jnp.logical_not(other))
            def _():
                pltpu.make_async_copy(src, dst, recv_sem).start()

    def exchange_kv(wait):
        for n, array in enumerate((k_in, v_in)):
            for d in range(KV_HEADS):
                d = (d + 1) % KV_HEADS
                k = (kv_head + d) % KV_HEADS
                cols = pl.ds(pl.multiple_of(k * HEAD_SIZE, HEAD_SIZE), HEAD_SIZE)
                send(array.at[:, cols], kv.at[n, b, my_half, my_rows, :],
                     first_send.at[n, d], row_recv.at[b],
                     (k // Y) * 2 + n, z * Y + k % Y, d == 0, wait)

    def exchange_q(wait):
        for half in range(2 // Y):
            for d in range(KV_HEADS):
                d = (d + 1) % KV_HEADS
                k = (kv_head + d) % KV_HEADS
                cols = pl.ds(pl.multiple_of((k * (2 // Y) + half) * width, width), width)
                core = half if Y == 1 else y
                send(q_in.at[:, cols], qbuf.at[my_half, my_rows, :],
                     first_send.at[2 + half, d], q_recv,
                     (k // Y) * 2 + core, z * Y + k % Y, d == 0, wait)

    def wait_row(row):
        pltpu.make_async_copy(kv.at[t, row], kv.at[t, row], row_recv.at[row]).wait()

    def wait_sibling(row):
        pltpu.make_async_copy(kv.at[1 - t, row], kv.at[1 - t, row], sib_recv.at[row]).wait()

    def pass_on(row, wait=False):
        def copy(head, blk, send_sem, recv_sem):
            c = pltpu.make_async_remote_copy(
                src_ref=kv.at[t, row], dst_ref=kv.at[t, row], send_sem=send_sem, recv_sem=recv_sem,
                device_id={"head": head, "blk": blk}, device_id_type=MESH)
            c.wait_send() if wait else c.start()

        j = row // Y

        @pl.when(jnp.logical_and(j <= z, z < Z - 1))
        def _():
            copy(h, b + Y, fwd_send.at[0, row], row_recv.at[row])

        @pl.when(jnp.logical_and(j >= z, z > 0))
        def _():
            copy(h, b - Y, fwd_send.at[1, row], row_recv.at[row])

        copy(sibling, b, sib_send.at[row], sib_recv.at[row])

    def seg_line(q_half):
        line = seg_buf[pl.ds(row_me, 1), :].astype(jnp.float32)
        return line[:, q_half * R:(q_half + 1) * R]

    def hide(col, line, extra=None):
        visible = jnp.concatenate([col] * (R // HEAD_SIZE), axis=1) == line
        if extra is not None:
            visible = jnp.logical_and(visible, extra)
        bias = jnp.where(visible, 0.0, MASKED)
        return jnp.concatenate([bias] * HQ, axis=1)

    def scores(keys, q_half):
        return jnp.dot(keys, qt[q_half], preferred_element_type=jnp.float32)

    def tile(s, bias, values_t):
        s = s + bias
        m = jnp.max(s, axis=0, keepdims=True)
        w = jnp.exp2((s - m) * SCALE)
        return (m, jnp.sum(w, axis=0, keepdims=True),
                jnp.dot(values_t, w.astype(jnp.bfloat16), preferred_element_type=jnp.float32))

    def merge(*states):
        m = functools.reduce(jnp.maximum, [x[0] for x in states])
        fades = [jnp.exp2((x[0] - m) * SCALE) for x in states]
        return (m, sum(x[1] * f for x, f in zip(states, fades)),
                sum(x[2] * f for x, f in zip(states, fades)))

    def load(which):
        return top[which], total[which], acc[which]

    def store(which, state):
        top[which], total[which], acc[which] = state

    def own():
        rows = lax.broadcasted_iota(jnp.int32, (R, R), 0)
        columns = lax.broadcasted_iota(jnp.int32, (R, R), 1)
        keys = [kv[0, row_me, half] for half in range(2)]
        values_t = [jnp.transpose(kv[1, row_me, half]) for half in range(2)]
        for half in range(2):
            for g in range(HQ):
                qt[half, :, g * R:(g + 1) * R] = jnp.transpose(qbuf[half, :, g * HEAD_SIZE:(g + 1) * HEAD_SIZE])
        s = [scores(keys[0], 0), scores(keys[1], 1), scores(keys[0], 1)]
        first = tile(s[0], hide(segc[row_me, 0], seg_line(0), rows <= columns), values_t[0])
        second = tile(s[1], hide(segc[row_me, 1], seg_line(1), rows <= columns), values_t[1])
        third = tile(s[2], hide(segc[row_me, 0], seg_line(1)), values_t[0])
        store(0, first)
        store(1, merge(second, third))

    def attend(row):
        which = (pos_buf[row, 0] > pos_buf[row_me, 0]).astype(jnp.int32)
        late = which == 1
        keys = kv[0, row, 0]
        values = kv[1, row, 0]
        col = segc[row, 0]
        s_a = scores(keys, 1)
        s_b = scores(jnp.where(late, kv[0, row, 1], keys), which)
        one = tile(s_a, hide(col, seg_line(1)), jnp.transpose(values))
        m, tot, a = tile(
            s_b, hide(jnp.where(late, segc[row, 1], col), jnp.where(late, seg_line(1), seg_line(0))),
            jnp.transpose(jnp.where(late, kv[1, row, 1], values)))
        early = merge(load(0), (jnp.where(late, MASKED, m), tot, a))
        later = merge(load(1), one, (jnp.where(late, m, MASKED), tot, a))
        store(0, early)
        store(1, later)

    def side(u, way, do):
        j = z + (1 + u // Y) * (2 * way - 1)

        @pl.when(jnp.logical_and(j >= 0, j < Z))
        def _():
            do(j * Y + u % Y)

    def arrive_row(row):
        wait_row(row)
        pass_on(row)

    def use_row(row):
        wait_sibling(row)
        attend(row)

    def arrive(u):
        side(u, 0, arrive_row)
        side(u, 1, arrive_row)

    exchange_kv(False)
    for copy in fetch:
        copy.wait()
    for r in range(Y):
        wait_row(z * Y + r)
        pass_on(z * Y + r)
    exchange_q(False)

    def column(row, c):
        line = seg_buf[pl.ds(row, 1), :].astype(jnp.float32)
        segc[row] = jnp.transpose(jnp.broadcast_to(line, (HEAD_SIZE, 2 * R))).reshape(2, R, HEAD_SIZE)
        return c

    lax.fori_loop(0, B, column, 0)

    units = (Z - 1) * Y
    between = jnp.logical_and(z > 0, z < Z - 1)
    ahead = jnp.where(between, 4, 2)
    for u in range(min(2, units)):
        arrive(u)
    pltpu.make_async_copy(qbuf, qbuf, q_recv).wait()
    for r in range(Y):
        wait_sibling(z * Y + r)
    own()

    def early(u):
        @pl.when(jnp.logical_and(between, u < units))
        def _():
            arrive(u)

    early(2)
    for r in range(1, Y):
        attend(z * Y + (t + r) % Y)
    early(3)

    def step(u, c):
        def each(way, c):
            side(u, way, use_row)
            return c

        lax.fori_loop(0, 2, each, 0)

        @pl.when(u + ahead < units)
        def _():
            arrive(u + ahead)

        return c

    lax.fori_loop(0, units, step, 0)

    slot = kv_head * (2 // Y) + (t if Y == 1 else 0)
    out_cols = pl.ds(pl.multiple_of(slot * width, width), width)

    def send_out(half, wait):
        for e in range(HH):
            e = (e + 1) % HH
            i = half * HH + (h + e) % HH
            i_half, i_rows = part(i)
            send(obuf.at[i_half, i_rows, :], out_ref.at[:, out_cols],
                 out_send.at[half, e], out_recv, i, row_me, True, wait)

    for half in range(2):
        for g in range(HQ):
            o = acc[half, :, g * R:(g + 1) * R] / total[half, :, g * R:(g + 1) * R]
            obuf[half, :, g * HEAD_SIZE:(g + 1) * HEAD_SIZE] = jnp.transpose(o).astype(jnp.bfloat16)
        send_out(half, False)

    exchange_kv(True)
    exchange_q(True)

    def drain(row, c):
        pass_on(row, True)
        return c

    lax.fori_loop(0, B, drain, 0)
    for half in range(2):
        send_out(half, True)
    pltpu.make_async_copy(out_ref, out_ref, out_recv).wait()


def local(queries, keys, values, position, segment):
    H, B = lax.axis_size("head"), lax.axis_size("blk")
    T = queries.shape[1]
    Y = 2 * KV_HEADS // H
    HQ = QUERY_HEADS // H
    R = position.shape[1] // 2
    pairs = B * (2 * R) ** 2 * HQ * 17 // 32
    out = pl.pallas_call(
        functools.partial(kernel, H, B),
        out_shape=jax.ShapeDtypeStruct((T, QUERY_HEADS * HEAD_SIZE), jnp.bfloat16),
        in_specs=[pl.BlockSpec(memory_space=pltpu.HBM)] * 5,
        out_specs=pl.BlockSpec(memory_space=pl.ANY),
        scratch_shapes=[
            pltpu.VMEM((2, R, HQ * HEAD_SIZE), jnp.bfloat16),
            pltpu.VMEM((2, B, 2, R, HEAD_SIZE), jnp.bfloat16),
            pltpu.VMEM((B, 2, R, HEAD_SIZE), jnp.float32),
            pltpu.VMEM((2, R, HQ * HEAD_SIZE), jnp.bfloat16),
            pltpu.VMEM((2, 1, HQ * R), jnp.float32),
            pltpu.VMEM((2, 1, HQ * R), jnp.float32),
            pltpu.VMEM((2, HEAD_SIZE, HQ * R), jnp.float32),
            pltpu.VMEM((2, HEAD_SIZE, HQ * R), jnp.bfloat16),
            pltpu.SMEM(position.shape, jnp.int32),
            pltpu.VMEM(segment.shape, jnp.int32),
            pltpu.SemaphoreType.DMA((2,)),
            pltpu.SemaphoreType.DMA((2 + 2 // Y, KV_HEADS)),
            pltpu.SemaphoreType.DMA,
            pltpu.SemaphoreType.DMA((B,)),
            pltpu.SemaphoreType.DMA((B,)),
            pltpu.SemaphoreType.DMA((2, B)),
            pltpu.SemaphoreType.DMA((B,)),
            pltpu.SemaphoreType.DMA((2, H // 2)),
            pltpu.SemaphoreType.DMA,
        ],
        compiler_params=pltpu.CompilerParams(
            collective_id=0, has_side_effects=True, vmem_limit_bytes=60 * 2**20
        ),
        cost_estimate=pl.CostEstimate(
            flops=4 * pairs * HEAD_SIZE, bytes_accessed=8 * T * QUERY_HEADS * HEAD_SIZE, transcendentals=pairs
        ),
    )(queries[0], keys[0], values[0], position, segment)
    return out[None]


def solution(mesh):
    return jax.shard_map(
        local,
        mesh=mesh,
        in_specs=(P("blk", "head", None), P("blk", "head", None), P("blk", "head", None), P(), P()),
        out_specs=P("blk", "head", None),
        check_vma=False,
    )
```

```python
import functools
import math

import jax
import jax.numpy as jnp
from jax import lax
from jax.experimental import pallas as pl
from jax.experimental.pallas import tpu as pltpu
from jax.sharding import PartitionSpec as P

QUERY_HEADS = 16
KV_HEADS = 4
HEAD_SIZE = 128
MASKED = -1e30
SCALE = math.log2(math.e) / math.sqrt(HEAD_SIZE)
MESH = pl.DeviceIdType.MESH


def kernel(H, B, q_in, k_in, v_in, pos_ref, seg_ref, out_ref,
           qbuf, kv, segc, obuf, top, total, acc, qt, pos_buf, seg_buf, small,
           first_send, q_recv, row_recv, sib_recv, fwd_send, sib_send, out_send, out_recv):
    Y = 2 * KV_HEADS // H
    Z = B // Y
    HQ = QUERY_HEADS // H
    HH = H // 2
    T = q_in.shape[0]
    R = qbuf.shape[1]
    width = HQ * HEAD_SIZE
    h = lax.axis_index("head")
    b = lax.axis_index("blk")
    chip, t = h // 2, h % 2
    z, y = b // Y, b % Y
    kv_head = chip * Y + y
    sibling = chip * 2 + 1 - t
    row_me = z * Y + t % Y

    fetch = [pltpu.make_async_copy(pos_ref, pos_buf, small.at[0]), pltpu.make_async_copy(seg_ref, seg_buf, small.at[1])]
    for copy in fetch:
        copy.start()

    barrier = pltpu.get_barrier_semaphore()
    for i in range(H):
        for r in range(Y):
            @pl.when(jnp.logical_or(h != i, y != r))
            def _():
                pl.semaphore_signal(barrier, inc=1, device_id={"head": i, "blk": z * Y + r}, device_id_type=MESH)

    @pl.when(z > 0)
    def _():
        pl.semaphore_signal(barrier, inc=1, device_id={"head": h, "blk": b - Y}, device_id_type=MESH)

    @pl.when(z < Z - 1)
    def _():
        pl.semaphore_signal(barrier, inc=1, device_id={"head": h, "blk": b + Y}, device_id_type=MESH)

    near = (z > 0).astype(jnp.int32) + (z < Z - 1).astype(jnp.int32)
    pl.semaphore_wait(barrier, H * Y - 1 + near)

    def part(i):
        return i // HH, pl.ds(pl.multiple_of((i % HH) * T, T), T)

    my_half, my_rows = part(h)

    def send(src, dst, send_sem, recv_sem, head, blk, may_be_me, wait=False):
        def remote():
            copy = pltpu.make_async_remote_copy(
                src_ref=src, dst_ref=dst, send_sem=send_sem, recv_sem=recv_sem,
                device_id={"head": head, "blk": blk}, device_id_type=MESH)
            copy.wait_send() if wait else copy.start()

        if not may_be_me:
            remote()
            return
        other = jnp.logical_or(head != h, blk != b)
        pl.when(other)(remote)
        if not wait:
            @pl.when(jnp.logical_not(other))
            def _():
                pltpu.make_async_copy(src, dst, recv_sem).start()

    def exchange_kv(wait):
        for n, array in enumerate((k_in, v_in)):
            for d in range(KV_HEADS):
                d = (d + 1) % KV_HEADS
                k = (kv_head + d) % KV_HEADS
                cols = pl.ds(pl.multiple_of(k * HEAD_SIZE, HEAD_SIZE), HEAD_SIZE)
                send(array.at[:, cols], kv.at[n, b, my_half, my_rows, :],
                     first_send.at[n, d], row_recv.at[b],
                     (k // Y) * 2 + n, z * Y + k % Y, d == 0, wait)

    def exchange_q(wait):
        for half in range(2 // Y):
            for d in range(KV_HEADS):
                d = (d + 1) % KV_HEADS
                k = (kv_head + d) % KV_HEADS
                cols = pl.ds(pl.multiple_of((k * (2 // Y) + half) * width, width), width)
                core = half if Y == 1 else y
                send(q_in.at[:, cols], qbuf.at[my_half, my_rows, :],
                     first_send.at[2 + half, d], q_recv,
                     (k // Y) * 2 + core, z * Y + k % Y, d == 0, wait)

    def wait_row(row):
        pltpu.make_async_copy(kv.at[t, row], kv.at[t, row], row_recv.at[row]).wait()

    def wait_sibling(row):
        pltpu.make_async_copy(kv.at[1 - t, row], kv.at[1 - t, row], sib_recv.at[row]).wait()

    def pass_on(row, wait=False):
        def copy(head, blk, send_sem, recv_sem):
            c = pltpu.make_async_remote_copy(
                src_ref=kv.at[t, row], dst_ref=kv.at[t, row], send_sem=send_sem, recv_sem=recv_sem,
                device_id={"head": head, "blk": blk}, device_id_type=MESH)
            c.wait_send() if wait else c.start()

        j = row // Y

        @pl.when(jnp.logical_and(j <= z, z < Z - 1))
        def _():
            copy(h, b + Y, fwd_send.at[0, row], row_recv.at[row])

        @pl.when(jnp.logical_and(j >= z, z > 0))
        def _():
            copy(h, b - Y, fwd_send.at[1, row], row_recv.at[row])

        copy(sibling, b, sib_send.at[row], sib_recv.at[row])

    def seg_line(q_half):
        line = seg_buf[pl.ds(row_me, 1), :].astype(jnp.float32)
        return line[:, q_half * R:(q_half + 1) * R]

    def hide(col, line, extra=None):
        visible = jnp.concatenate([col] * (R // HEAD_SIZE), axis=1) == line
        if extra is not None:
            visible = jnp.logical_and(visible, extra)
        bias = jnp.where(visible, 0.0, MASKED)
        return jnp.concatenate([bias] * HQ, axis=1)

    def scores(keys, q_half):
        return jnp.dot(keys, qt[q_half], preferred_element_type=jnp.float32)

    def tile(s, bias, values_t):
        s = s + bias
        m = jnp.max(s, axis=0, keepdims=True)
        w = jnp.exp2((s - m) * SCALE)
        return (m, jnp.sum(w, axis=0, keepdims=True),
                jnp.dot(values_t, w.astype(jnp.bfloat16), preferred_element_type=jnp.float32))

    def merge(*states):
        m = functools.reduce(jnp.maximum, [x[0] for x in states])
        fades = [jnp.exp2((x[0] - m) * SCALE) for x in states]
        return (m, sum(x[1] * f for x, f in zip(states, fades)),
                sum(x[2] * f for x, f in zip(states, fades)))

    def load(which):
        return top[which], total[which], acc[which]

    def store(which, state):
        top[which], total[which], acc[which] = state

    def own():
        rows = lax.broadcasted_iota(jnp.int32, (R, R), 0)
        columns = lax.broadcasted_iota(jnp.int32, (R, R), 1)
        keys = [kv[0, row_me, half] for half in range(2)]
        values_t = [jnp.transpose(kv[1, row_me, half]) for half in range(2)]
        for half in range(2):
            for g in range(HQ):
                qt[half, :, g * R:(g + 1) * R] = jnp.transpose(qbuf[half, :, g * HEAD_SIZE:(g + 1) * HEAD_SIZE])
        s = [scores(keys[0], 0), scores(keys[1], 1), scores(keys[0], 1)]
        first = tile(s[0], hide(segc[row_me, 0], seg_line(0), rows <= columns), values_t[0])
        second = tile(s[1], hide(segc[row_me, 1], seg_line(1), rows <= columns), values_t[1])
        third = tile(s[2], hide(segc[row_me, 0], seg_line(1)), values_t[0])
        store(0, first)
        store(1, merge(second, third))

    def choose(row):
        which = (pos_buf[row, 0] > pos_buf[row_me, 0]).astype(jnp.int32)
        return which, which == 1

    def fixed_scores(row):
        return scores(kv[0, row, 0], 1)

    def fixed_tile(row, s):
        return tile(s, hide(segc[row, 0], seg_line(1)), jnp.transpose(kv[1, row, 0]))

    def other_scores(row):
        which, late = choose(row)
        return scores(jnp.where(late, kv[0, row, 1], kv[0, row, 0]), which)

    def other_tile(row, s):
        which, late = choose(row)
        col = jnp.where(late, segc[row, 1], segc[row, 0])
        m, tot, a = tile(s, hide(col, jnp.where(late, seg_line(1), seg_line(0))),
                         jnp.transpose(jnp.where(late, kv[1, row, 1], kv[1, row, 0])))
        return (jnp.where(late, MASKED, m), tot, a), (jnp.where(late, m, MASKED), tot, a)

    def attend(row):
        s_a, s_b = fixed_scores(row), other_scores(row)
        one = fixed_tile(row, s_a)
        to_early, to_later = other_tile(row, s_b)
        early = merge(load(0), to_early)
        later = merge(load(1), one, to_later)
        store(0, early)
        store(1, later)

    def attend_other(row):
        wait_sibling(row)
        to_early, to_later = other_tile(row, other_scores(row))
        early, later = merge(load(0), to_early), merge(load(1), to_later)
        store(0, early)
        store(1, later)

    def attend_fixed(row):
        store(1, merge(load(1), fixed_tile(row, fixed_scores(row))))

    def side(u, way, do):
        j = z + (1 + u // Y) * (2 * way - 1)

        @pl.when(jnp.logical_and(j >= 0, j < Z))
        def _():
            do(j * Y + u % Y)

    def arrive_row(row):
        wait_row(row)
        pass_on(row)

    def use_row(row):
        wait_sibling(row)
        attend(row)

    def arrive(u):
        side(u, 0, arrive_row)
        side(u, 1, arrive_row)

    exchange_kv(False)
    for copy in fetch:
        copy.wait()
    for r in range(Y):
        wait_row(z * Y + r)
        pass_on(z * Y + r)
    exchange_q(False)

    def column(row, c):
        line = seg_buf[pl.ds(row, 1), :].astype(jnp.float32)
        segc[row] = jnp.transpose(jnp.broadcast_to(line, (HEAD_SIZE, 2 * R))).reshape(2, R, HEAD_SIZE)
        return c

    lax.fori_loop(0, B, column, 0)

    units = (Z - 1) * Y
    between = jnp.logical_and(z > 0, z < Z - 1)
    ahead = jnp.where(between, 4, 2)
    for u in range(min(2, units)):
        arrive(u)
    pltpu.make_async_copy(qbuf, qbuf, q_recv).wait()
    for r in range(Y):
        wait_sibling(z * Y + r)
    own()

    def early(u):
        @pl.when(jnp.logical_and(between, u < units))
        def _():
            arrive(u)

    early(2)
    for r in range(1, Y):
        attend(z * Y + (t + r) % Y)
    early(3)

    def step(u, c):
        def each(way, c):
            side(u, way, use_row)
            return c

        lax.fori_loop(0, 2, each, 0)

        @pl.when(u + ahead < units)
        def _():
            arrive(u + ahead)

        return c

    last = jnp.maximum(z, Z - 1 - z) * Y - 1
    lax.fori_loop(0, last, step, 0)

    def each_side(do):
        def each(way, c):
            side(last, way, do)
            return c

        lax.fori_loop(0, 2, each, 0)

    each_side(attend_other)

    slot = kv_head * (2 // Y) + (t if Y == 1 else 0)
    out_cols = pl.ds(pl.multiple_of(slot * width, width), width)

    def send_out(half, wait):
        for e in range(HH):
            e = (e + 1) % HH
            i = half * HH + (h + e) % HH
            i_half, i_rows = part(i)
            send(obuf.at[i_half, i_rows, :], out_ref.at[:, out_cols],
                 out_send.at[half, e], out_recv, i, row_me, True, wait)

    for half in range(2):
        if half == 1:
            each_side(attend_fixed)
        outs = acc[half] * (1.0 / total[half])
        for g in range(HQ):
            o = jnp.transpose(outs[:, g * R:(g + 1) * R]).astype(jnp.bfloat16)
            obuf[half, :, g * HEAD_SIZE:(g + 1) * HEAD_SIZE] = o
        send_out(half, False)

    exchange_kv(True)
    exchange_q(True)

    def drain(row, c):
        pass_on(row, True)
        return c

    lax.fori_loop(0, B, drain, 0)
    for half in range(2):
        send_out(half, True)
    pltpu.make_async_copy(out_ref, out_ref, out_recv).wait()


def local(queries, keys, values, position, segment):
    H, B = lax.axis_size("head"), lax.axis_size("blk")
    T = queries.shape[1]
    Y = 2 * KV_HEADS // H
    HQ = QUERY_HEADS // H
    R = position.shape[1] // 2
    pairs = B * (2 * R) ** 2 * HQ * 17 // 32
    out = pl.pallas_call(
        functools.partial(kernel, H, B),
        out_shape=jax.ShapeDtypeStruct((T, QUERY_HEADS * HEAD_SIZE), jnp.bfloat16),
        in_specs=[pl.BlockSpec(memory_space=pltpu.HBM)] * 5,
        out_specs=pl.BlockSpec(memory_space=pl.ANY),
        scratch_shapes=[
            pltpu.VMEM((2, R, HQ * HEAD_SIZE), jnp.bfloat16),
            pltpu.VMEM((2, B, 2, R, HEAD_SIZE), jnp.bfloat16),
            pltpu.VMEM((B, 2, R, HEAD_SIZE), jnp.float32),
            pltpu.VMEM((2, R, HQ * HEAD_SIZE), jnp.bfloat16),
            pltpu.VMEM((2, 1, HQ * R), jnp.float32),
            pltpu.VMEM((2, 1, HQ * R), jnp.float32),
            pltpu.VMEM((2, HEAD_SIZE, HQ * R), jnp.float32),
            pltpu.VMEM((2, HEAD_SIZE, HQ * R), jnp.bfloat16),
            pltpu.SMEM(position.shape, jnp.int32),
            pltpu.VMEM(segment.shape, jnp.int32),
            pltpu.SemaphoreType.DMA((2,)),
            pltpu.SemaphoreType.DMA((2 + 2 // Y, KV_HEADS)),
            pltpu.SemaphoreType.DMA,
            pltpu.SemaphoreType.DMA((B,)),
            pltpu.SemaphoreType.DMA((B,)),
            pltpu.SemaphoreType.DMA((2, B)),
            pltpu.SemaphoreType.DMA((B,)),
            pltpu.SemaphoreType.DMA((2, H // 2)),
            pltpu.SemaphoreType.DMA,
        ],
        compiler_params=pltpu.CompilerParams(
            collective_id=0, has_side_effects=True, vmem_limit_bytes=60 * 2**20
        ),
        cost_estimate=pl.CostEstimate(
            flops=4 * pairs * HEAD_SIZE, bytes_accessed=8 * T * QUERY_HEADS * HEAD_SIZE, transcendentals=pairs
        ),
    )(queries[0], keys[0], values[0], position, segment)
    return out[None]


def solution(mesh):
    return jax.shard_map(
        local,
        mesh=mesh,
        in_specs=(P("blk", "head", None), P("blk", "head", None), P("blk", "head", None), P(), P()),
        out_specs=P("blk", "head", None),
        check_vma=False,
    )
```

```python
import functools
import math

import jax
import jax.numpy as jnp
from jax import lax
from jax.experimental import pallas as pl
from jax.experimental.pallas import tpu as pltpu
from jax.sharding import PartitionSpec as P

QUERY_HEADS = 16
KV_HEADS = 4
HEAD_SIZE = 128
MASKED = -1e30
SCALE = math.log2(math.e) / math.sqrt(HEAD_SIZE)
MESH = pl.DeviceIdType.MESH


def kernel(H, B, q_in, k_in, v_in, pos_ref, seg_ref, out_ref,
           qbuf, kv, segc, obuf, top, total, acc, qt, pos_buf, seg_buf, small,
           first_send, q_recv, row_recv, sib_recv, fwd_send, sib_send, out_send, out_recv):
    Y = 2 * KV_HEADS // H
    Z = B // Y
    HQ = QUERY_HEADS // H
    HH = H // 2
    T = q_in.shape[0]
    R = qbuf.shape[1]
    width = HQ * HEAD_SIZE
    h = lax.axis_index("head")
    b = lax.axis_index("blk")
    chip, t = h // 2, h % 2
    z, y = b // Y, b % Y
    kv_head = chip * Y + y
    sibling = chip * 2 + 1 - t
    row_me = z * Y + t % Y

    fetch = [pltpu.make_async_copy(pos_ref, pos_buf, small.at[0]), pltpu.make_async_copy(seg_ref, seg_buf, small.at[1])]
    for copy in fetch:
        copy.start()

    barrier = pltpu.get_barrier_semaphore()
    for i in range(H):
        for r in range(Y):
            @pl.when(jnp.logical_or(h != i, y != r))
            def _():
                pl.semaphore_signal(barrier, inc=1, device_id={"head": i, "blk": z * Y + r}, device_id_type=MESH)

    @pl.when(z > 0)
    def _():
        pl.semaphore_signal(barrier, inc=1, device_id={"head": h, "blk": b - Y}, device_id_type=MESH)

    @pl.when(z < Z - 1)
    def _():
        pl.semaphore_signal(barrier, inc=1, device_id={"head": h, "blk": b + Y}, device_id_type=MESH)

    near = (z > 0).astype(jnp.int32) + (z < Z - 1).astype(jnp.int32)
    pl.semaphore_wait(barrier, H * Y - 1 + near)

    def part(i):
        return i // HH, pl.ds(pl.multiple_of((i % HH) * T, T), T)

    my_half, my_rows = part(h)

    def send(src, dst, send_sem, recv_sem, head, blk, may_be_me, wait=False):
        def remote():
            copy = pltpu.make_async_remote_copy(
                src_ref=src, dst_ref=dst, send_sem=send_sem, recv_sem=recv_sem,
                device_id={"head": head, "blk": blk}, device_id_type=MESH)
            copy.wait_send() if wait else copy.start()

        if not may_be_me:
            remote()
            return
        other = jnp.logical_or(head != h, blk != b)
        pl.when(other)(remote)
        if not wait:
            @pl.when(jnp.logical_not(other))
            def _():
                pltpu.make_async_copy(src, dst, recv_sem).start()

    def exchange_kv(wait):
        for n, array in enumerate((k_in, v_in)):
            for d in range(KV_HEADS):
                d = (d + 1) % KV_HEADS
                k = (kv_head + d) % KV_HEADS
                cols = pl.ds(pl.multiple_of(k * HEAD_SIZE, HEAD_SIZE), HEAD_SIZE)
                send(array.at[:, cols], kv.at[n, b, my_half, my_rows, :],
                     first_send.at[n, d], row_recv.at[b],
                     (k // Y) * 2 + n, z * Y + k % Y, d == 0, wait)

    def exchange_q(wait):
        for half in range(2 // Y):
            for d in range(KV_HEADS):
                d = (d + 1) % KV_HEADS
                k = (kv_head + d) % KV_HEADS
                cols = pl.ds(pl.multiple_of((k * (2 // Y) + half) * width, width), width)
                core = half if Y == 1 else y
                send(q_in.at[:, cols], qbuf.at[my_half, my_rows, :],
                     first_send.at[2 + half, d], q_recv,
                     (k // Y) * 2 + core, z * Y + k % Y, d == 0, wait)

    def wait_row(row):
        pltpu.make_async_copy(kv.at[t, row], kv.at[t, row], row_recv.at[row]).wait()

    def wait_sibling(row):
        pltpu.make_async_copy(kv.at[1 - t, row], kv.at[1 - t, row], sib_recv.at[row]).wait()

    def pass_on(row, wait=False):
        def copy(head, blk, send_sem, recv_sem):
            c = pltpu.make_async_remote_copy(
                src_ref=kv.at[t, row], dst_ref=kv.at[t, row], send_sem=send_sem, recv_sem=recv_sem,
                device_id={"head": head, "blk": blk}, device_id_type=MESH)
            c.wait_send() if wait else c.start()

        j = row // Y

        @pl.when(jnp.logical_and(j <= z, z < Z - 1))
        def _():
            copy(h, b + Y, fwd_send.at[0, row], row_recv.at[row])

        @pl.when(jnp.logical_and(j >= z, z > 0))
        def _():
            copy(h, b - Y, fwd_send.at[1, row], row_recv.at[row])

        copy(sibling, b, sib_send.at[row], sib_recv.at[row])

    def seg_line(q_half):
        line = seg_buf[pl.ds(row_me, 1), :].astype(jnp.float32)
        return line[:, q_half * R:(q_half + 1) * R]

    def hide(col, line, extra=None):
        visible = jnp.concatenate([col] * (R // HEAD_SIZE), axis=1) == line
        if extra is not None:
            visible = jnp.logical_and(visible, extra)
        bias = jnp.where(visible, 0.0, MASKED)
        return jnp.concatenate([bias] * HQ, axis=1)

    def scores(keys, q_half):
        return jnp.dot(keys, qt[q_half], preferred_element_type=jnp.float32)

    def tile(s, bias, values_t):
        s = s + bias
        m = jnp.max(s, axis=0, keepdims=True)
        w = jnp.exp2((s - m) * SCALE)
        return (m, jnp.sum(w, axis=0, keepdims=True),
                jnp.dot(values_t, w.astype(jnp.bfloat16), preferred_element_type=jnp.float32))

    def merge(*states):
        m = functools.reduce(jnp.maximum, [x[0] for x in states])
        fades = [jnp.exp2((x[0] - m) * SCALE) for x in states]
        return (m, sum(x[1] * f for x, f in zip(states, fades)),
                sum(x[2] * f for x, f in zip(states, fades)))

    def load(which):
        return top[which], total[which], acc[which]

    def store(which, state):
        top[which], total[which], acc[which] = state

    def own():
        rows = lax.broadcasted_iota(jnp.int32, (R, R), 0)
        columns = lax.broadcasted_iota(jnp.int32, (R, R), 1)
        keys = [kv[0, row_me, half] for half in range(2)]
        values_t = [jnp.transpose(kv[1, row_me, half]) for half in range(2)]
        for half in range(2):
            for g in range(HQ):
                qt[half, :, g * R:(g + 1) * R] = jnp.transpose(qbuf[half, :, g * HEAD_SIZE:(g + 1) * HEAD_SIZE])
        s = [scores(keys[0], 0), scores(keys[1], 1), scores(keys[0], 1)]
        first = tile(s[0], hide(segc[row_me, 0], seg_line(0), rows <= columns), values_t[0])
        second = tile(s[1], hide(segc[row_me, 1], seg_line(1), rows <= columns), values_t[1])
        third = tile(s[2], hide(segc[row_me, 0], seg_line(1)), values_t[0])
        store(0, first)
        store(1, merge(second, third))

    def choose(row):
        which = (pos_buf[row, 0] > pos_buf[row_me, 0]).astype(jnp.int32)
        return which, which == 1

    def fixed_scores(row):
        return scores(kv[0, row, 0], 1)

    def fixed_tile(row, s):
        return tile(s, hide(segc[row, 0], seg_line(1)), jnp.transpose(kv[1, row, 0]))

    def other_scores(row):
        which, late = choose(row)
        return scores(jnp.where(late, kv[0, row, 1], kv[0, row, 0]), which)

    def other_tile(row, s):
        which, late = choose(row)
        col = jnp.where(late, segc[row, 1], segc[row, 0])
        m, tot, a = tile(s, hide(col, jnp.where(late, seg_line(1), seg_line(0))),
                         jnp.transpose(jnp.where(late, kv[1, row, 1], kv[1, row, 0])))
        return (jnp.where(late, MASKED, m), tot, a), (jnp.where(late, m, MASKED), tot, a)

    def attend(row):
        s_a, s_b = fixed_scores(row), other_scores(row)
        one = fixed_tile(row, s_a)
        to_early, to_later = other_tile(row, s_b)
        early = merge(load(0), to_early)
        later = merge(load(1), one, to_later)
        store(0, early)
        store(1, later)

    def attend_other(row):
        wait_sibling(row)
        to_early, to_later = other_tile(row, other_scores(row))
        early, later = merge(load(0), to_early), merge(load(1), to_later)
        store(0, early)
        store(1, later)

    def attend_fixed(row):
        store(1, merge(load(1), fixed_tile(row, fixed_scores(row))))

    def side(u, way, do):
        j = z + (1 + u // Y) * (2 * way - 1)

        @pl.when(jnp.logical_and(j >= 0, j < Z))
        def _():
            do(j * Y + u % Y)

    def arrive_row(row):
        wait_row(row)
        pass_on(row)

    def use_row(row):
        wait_sibling(row)
        attend(row)

    def arrive(u):
        side(u, 0, arrive_row)
        side(u, 1, arrive_row)

    exchange_kv(False)
    exchange_q(False)
    for copy in fetch:
        copy.wait()
    for r in range(Y):
        wait_row(z * Y + r)
        pass_on(z * Y + r)

    def column(row, c):
        line = seg_buf[pl.ds(row, 1), :].astype(jnp.float32)
        segc[row] = jnp.transpose(jnp.broadcast_to(line, (HEAD_SIZE, 2 * R))).reshape(2, R, HEAD_SIZE)
        return c

    lax.fori_loop(0, B, column, 0)

    units = (Z - 1) * Y
    between = jnp.logical_and(z > 0, z < Z - 1)
    ahead = jnp.where(between, 4, 2)
    for u in range(min(2, units)):
        arrive(u)
    pltpu.make_async_copy(qbuf, qbuf, q_recv).wait()
    for r in range(Y):
        wait_sibling(z * Y + r)
    own()

    def early(u):
        @pl.when(jnp.logical_and(between, u < units))
        def _():
            arrive(u)

    early(2)
    for r in range(1, Y):
        attend(z * Y + (t + r) % Y)
    early(3)

    def step(u, c):
        def each(way, c):
            side(u, way, use_row)
            return c

        lax.fori_loop(0, 2, each, 0)

        @pl.when(u + ahead < units)
        def _():
            arrive(u + ahead)

        return c

    last = jnp.maximum(z, Z - 1 - z) * Y - 1
    lax.fori_loop(0, last, step, 0)

    def each_side(do):
        def each(way, c):
            side(last, way, do)
            return c

        lax.fori_loop(0, 2, each, 0)

    each_side(attend_other)

    slot = kv_head * (2 // Y) + (t if Y == 1 else 0)
    out_cols = pl.ds(pl.multiple_of(slot * width, width), width)

    def send_out(half, wait):
        for e in range(HH):
            i = half * HH + (h + e) % HH
            i_half, i_rows = part(i)
            send(obuf.at[i_half, i_rows, :], out_ref.at[:, out_cols],
                 out_send.at[half, e], out_recv, i, row_me, True, wait)

    for half in range(2):
        if half == 1:
            each_side(attend_fixed)
        outs = acc[half] * (1.0 / total[half])
        for g in range(HQ):
            o = jnp.transpose(outs[:, g * R:(g + 1) * R]).astype(jnp.bfloat16)
            obuf[half, :, g * HEAD_SIZE:(g + 1) * HEAD_SIZE] = o
        send_out(half, False)

    exchange_kv(True)
    exchange_q(True)

    def drain(row, c):
        pass_on(row, True)
        return c

    lax.fori_loop(0, B, drain, 0)
    for half in range(2):
        send_out(half, True)
    pltpu.make_async_copy(out_ref, out_ref, out_recv).wait()


def local(queries, keys, values, position, segment):
    H, B = lax.axis_size("head"), lax.axis_size("blk")
    T = queries.shape[1]
    Y = 2 * KV_HEADS // H
    HQ = QUERY_HEADS // H
    R = position.shape[1] // 2
    pairs = B * (2 * R) ** 2 * HQ * 17 // 32
    out = pl.pallas_call(
        functools.partial(kernel, H, B),
        out_shape=jax.ShapeDtypeStruct((T, QUERY_HEADS * HEAD_SIZE), jnp.bfloat16),
        in_specs=[pl.BlockSpec(memory_space=pltpu.HBM)] * 5,
        out_specs=pl.BlockSpec(memory_space=pl.ANY),
        scratch_shapes=[
            pltpu.VMEM((2, R, HQ * HEAD_SIZE), jnp.bfloat16),
            pltpu.VMEM((2, B, 2, R, HEAD_SIZE), jnp.bfloat16),
            pltpu.VMEM((B, 2, R, HEAD_SIZE), jnp.float32),
            pltpu.VMEM((2, R, HQ * HEAD_SIZE), jnp.bfloat16),
            pltpu.VMEM((2, 1, HQ * R), jnp.float32),
            pltpu.VMEM((2, 1, HQ * R), jnp.float32),
            pltpu.VMEM((2, HEAD_SIZE, HQ * R), jnp.float32),
            pltpu.VMEM((2, HEAD_SIZE, HQ * R), jnp.bfloat16),
            pltpu.SMEM(position.shape, jnp.int32),
            pltpu.VMEM(segment.shape, jnp.int32),
            pltpu.SemaphoreType.DMA((2,)),
            pltpu.SemaphoreType.DMA((2 + 2 // Y, KV_HEADS)),
            pltpu.SemaphoreType.DMA,
            pltpu.SemaphoreType.DMA((B,)),
            pltpu.SemaphoreType.DMA((B,)),
            pltpu.SemaphoreType.DMA((2, B)),
            pltpu.SemaphoreType.DMA((B,)),
            pltpu.SemaphoreType.DMA((2, H // 2)),
            pltpu.SemaphoreType.DMA,
        ],
        compiler_params=pltpu.CompilerParams(
            collective_id=0, has_side_effects=True, vmem_limit_bytes=60 * 2**20
        ),
        cost_estimate=pl.CostEstimate(
            flops=4 * pairs * HEAD_SIZE, bytes_accessed=8 * T * QUERY_HEADS * HEAD_SIZE, transcendentals=pairs
        ),
    )(queries[0], keys[0], values[0], position, segment)
    return out[None]


def solution(mesh):
    return jax.shard_map(
        local,
        mesh=mesh,
        in_specs=(P("blk", "head", None), P("blk", "head", None), P("blk", "head", None), P(), P()),
        out_specs=P("blk", "head", None),
        check_vma=False,
    )
```

```python
import functools
import math

import jax
import jax.numpy as jnp
from jax import lax
from jax.experimental import pallas as pl
from jax.experimental.pallas import tpu as pltpu
from jax.sharding import PartitionSpec as P

QUERY_HEADS = 16
KV_HEADS = 4
HEAD_SIZE = 128
MASKED = -1e30
SCALE = math.log2(math.e) / math.sqrt(HEAD_SIZE)
MESH = pl.DeviceIdType.MESH


def kernel(H, B, q_in, k_in, v_in, pos_ref, seg_ref, out_ref,
           qbuf, kv, segc, obuf, top, total, acc, qt, pos_buf, seg_buf, small,
           first_send, q_recv, row_recv, sib_recv, fwd_send, sib_send, out_send, out_recv):
    Y = 2 * KV_HEADS // H
    Z = B // Y
    HQ = QUERY_HEADS // H
    HH = H // 2
    T = q_in.shape[0]
    R = qbuf.shape[1]
    width = HQ * HEAD_SIZE
    h = lax.axis_index("head")
    b = lax.axis_index("blk")
    chip, t = h // 2, h % 2
    z, y = b // Y, b % Y
    kv_head = chip * Y + y
    sibling = chip * 2 + 1 - t
    row_me = z * Y + t % Y

    fetch = [pltpu.make_async_copy(pos_ref, pos_buf, small.at[0]), pltpu.make_async_copy(seg_ref, seg_buf, small.at[1])]
    for copy in fetch:
        copy.start()

    barrier = pltpu.get_barrier_semaphore()
    for i in range(H):
        for r in range(Y):
            @pl.when(jnp.logical_or(h != i, y != r))
            def _():
                pl.semaphore_signal(barrier, inc=1, device_id={"head": i, "blk": z * Y + r}, device_id_type=MESH)

    @pl.when(z > 0)
    def _():
        pl.semaphore_signal(barrier, inc=1, device_id={"head": h, "blk": b - Y}, device_id_type=MESH)

    @pl.when(z < Z - 1)
    def _():
        pl.semaphore_signal(barrier, inc=1, device_id={"head": h, "blk": b + Y}, device_id_type=MESH)

    near = (z > 0).astype(jnp.int32) + (z < Z - 1).astype(jnp.int32)
    pl.semaphore_wait(barrier, H * Y - 1 + near)

    def part(i):
        return i // HH, pl.ds(pl.multiple_of((i % HH) * T, T), T)

    my_half, my_rows = part(h)

    def send(src, dst, send_sem, recv_sem, head, blk, may_be_me, wait=False):
        def remote():
            copy = pltpu.make_async_remote_copy(
                src_ref=src, dst_ref=dst, send_sem=send_sem, recv_sem=recv_sem,
                device_id={"head": head, "blk": blk}, device_id_type=MESH)
            copy.wait_send() if wait else copy.start()

        if not may_be_me:
            remote()
            return
        other = jnp.logical_or(head != h, blk != b)
        pl.when(other)(remote)
        if not wait:
            @pl.when(jnp.logical_not(other))
            def _():
                pltpu.make_async_copy(src, dst, recv_sem).start()

    def exchange_kv(wait):
        for n, array in enumerate((k_in, v_in)):
            for d in range(KV_HEADS):
                d = (d + 1) % KV_HEADS
                k = (kv_head + d) % KV_HEADS
                cols = pl.ds(pl.multiple_of(k * HEAD_SIZE, HEAD_SIZE), HEAD_SIZE)
                send(array.at[:, cols], kv.at[n, b, my_half, my_rows, :],
                     first_send.at[n, d], row_recv.at[b],
                     (k // Y) * 2 + n, z * Y + k % Y, d == 0, wait)

    def exchange_q(wait):
        for half in range(2 // Y):
            for d in range(KV_HEADS):
                d = (d + 1) % KV_HEADS
                k = (kv_head + d) % KV_HEADS
                cols = pl.ds(pl.multiple_of((k * (2 // Y) + half) * width, width), width)
                core = half if Y == 1 else y
                send(q_in.at[:, cols], qbuf.at[my_half, my_rows, :],
                     first_send.at[2 + half, d], q_recv,
                     (k // Y) * 2 + core, z * Y + k % Y, d == 0, wait)

    def wait_row(row):
        pltpu.make_async_copy(kv.at[t, row], kv.at[t, row], row_recv.at[row]).wait()

    def wait_sibling(row):
        pltpu.make_async_copy(kv.at[1 - t, row], kv.at[1 - t, row], sib_recv.at[row]).wait()

    def pass_on(row, wait=False):
        def copy(head, blk, send_sem, recv_sem):
            c = pltpu.make_async_remote_copy(
                src_ref=kv.at[t, row], dst_ref=kv.at[t, row], send_sem=send_sem, recv_sem=recv_sem,
                device_id={"head": head, "blk": blk}, device_id_type=MESH)
            c.wait_send() if wait else c.start()

        j = row // Y

        @pl.when(jnp.logical_and(j <= z, z < Z - 1))
        def _():
            copy(h, b + Y, fwd_send.at[0, row], row_recv.at[row])

        @pl.when(jnp.logical_and(j >= z, z > 0))
        def _():
            copy(h, b - Y, fwd_send.at[1, row], row_recv.at[row])

        copy(sibling, b, sib_send.at[row], sib_recv.at[row])

    def seg_line(q_half):
        line = seg_buf[pl.ds(row_me, 1), :].astype(jnp.float32)
        return line[:, q_half * R:(q_half + 1) * R]

    def hide(col, line, extra=None):
        visible = jnp.concatenate([col] * (R // HEAD_SIZE), axis=1) == line
        if extra is not None:
            visible = jnp.logical_and(visible, extra)
        bias = jnp.where(visible, 0.0, MASKED)
        return jnp.concatenate([bias] * HQ, axis=1)

    def scores(keys, q_half):
        return jnp.dot(keys, qt[q_half], preferred_element_type=jnp.float32)

    def tile(s, bias, values_t):
        s = s + bias
        m = jnp.max(s, axis=0, keepdims=True)
        w = jnp.exp2((s - m) * SCALE)
        return (m, jnp.sum(w, axis=0, keepdims=True),
                jnp.dot(values_t, w.astype(jnp.bfloat16), preferred_element_type=jnp.float32))

    def merge(*states):
        m = functools.reduce(jnp.maximum, [x[0] for x in states])
        fades = [jnp.exp2((x[0] - m) * SCALE) for x in states]
        return (m, sum(x[1] * f for x, f in zip(states, fades)),
                sum(x[2] * f for x, f in zip(states, fades)))

    def load(which):
        return top[which], total[which], acc[which]

    def store(which, state):
        top[which], total[which], acc[which] = state

    def own():
        rows = lax.broadcasted_iota(jnp.int32, (R, R), 0)
        columns = lax.broadcasted_iota(jnp.int32, (R, R), 1)
        keys = [kv[0, row_me, half] for half in range(2)]
        values_t = [jnp.transpose(kv[1, row_me, half]) for half in range(2)]
        for half in range(2):
            for g in range(HQ):
                qt[half, :, g * R:(g + 1) * R] = jnp.transpose(qbuf[half, :, g * HEAD_SIZE:(g + 1) * HEAD_SIZE])
        s = [scores(keys[0], 0), scores(keys[1], 1), scores(keys[0], 1)]
        first = tile(s[0], hide(segc[row_me, 0], seg_line(0), rows <= columns), values_t[0])
        second = tile(s[1], hide(segc[row_me, 1], seg_line(1), rows <= columns), values_t[1])
        third = tile(s[2], hide(segc[row_me, 0], seg_line(1)), values_t[0])
        store(0, first)
        store(1, merge(second, third))

    def choose(row):
        which = (pos_buf[row, 0] > pos_buf[row_me, 0]).astype(jnp.int32)
        return which, which == 1

    def fixed_scores(row):
        return scores(kv[0, row, 0], 1)

    def fixed_tile(row, s):
        return tile(s, hide(segc[row, 0], seg_line(1)), jnp.transpose(kv[1, row, 0]))

    def other_scores(row):
        which, late = choose(row)
        return scores(jnp.where(late, kv[0, row, 1], kv[0, row, 0]), which)

    def other_tile(row, s):
        which, late = choose(row)
        col = jnp.where(late, segc[row, 1], segc[row, 0])
        m, tot, a = tile(s, hide(col, jnp.where(late, seg_line(1), seg_line(0))),
                         jnp.transpose(jnp.where(late, kv[1, row, 1], kv[1, row, 0])))
        return (jnp.where(late, MASKED, m), tot, a), (jnp.where(late, m, MASKED), tot, a)

    def attend(row):
        s_a, s_b = fixed_scores(row), other_scores(row)
        one = fixed_tile(row, s_a)
        to_early, to_later = other_tile(row, s_b)
        early = merge(load(0), to_early)
        later = merge(load(1), one, to_later)
        store(0, early)
        store(1, later)

    def attend_other(row):
        wait_sibling(row)
        to_early, to_later = other_tile(row, other_scores(row))
        early, later = merge(load(0), to_early), merge(load(1), to_later)
        store(0, early)
        store(1, later)

    def attend_fixed(row):
        store(1, merge(load(1), fixed_tile(row, fixed_scores(row))))

    def side(u, way, do):
        j = z + (1 + u // Y) * (2 * way - 1)

        @pl.when(jnp.logical_and(jnp.logical_and(j >= 0, j < Z), u >= 0))
        def _():
            do(j * Y + u % Y)

    def arrive_row(row):
        wait_row(row)
        pass_on(row)

    def use_row(row):
        wait_sibling(row)
        attend(row)

    def arrive(u):
        side(u, 0, arrive_row)
        side(u, 1, arrive_row)

    exchange_kv(False)
    exchange_q(False)
    for copy in fetch:
        copy.wait()
    for r in range(Y):
        wait_row(z * Y + r)
        pass_on(z * Y + r)

    def column(row, c):
        line = seg_buf[pl.ds(row, 1), :].astype(jnp.float32)
        segc[row] = jnp.transpose(jnp.broadcast_to(line, (HEAD_SIZE, 2 * R))).reshape(2, R, HEAD_SIZE)
        return c

    lax.fori_loop(0, B, column, 0)

    units = (Z - 1) * Y
    between = jnp.logical_and(z > 0, z < Z - 1)
    ahead = jnp.where(between, 4, 2)
    for u in range(min(2, units)):
        arrive(u)
    pltpu.make_async_copy(qbuf, qbuf, q_recv).wait()
    for r in range(Y):
        wait_sibling(z * Y + r)
    own()

    def early(u):
        @pl.when(jnp.logical_and(between, u < units))
        def _():
            arrive(u)

    early(2)
    for r in range(1, Y):
        attend(z * Y + (t + r) % Y)
    early(3)

    def step(u, c):
        def each(way, c):
            side(u, way, use_row)
            return c

        lax.fori_loop(0, 2, each, 0)

        @pl.when(u + ahead < units)
        def _():
            arrive(u + ahead)

        return c

    last = jnp.maximum(z, Z - 1 - z) * Y - 1
    held = 3
    lax.fori_loop(0, jnp.maximum(last + 1 - held, 0), step, 0)

    def tail(k, way, do):
        side(last + 1 - held + k, way, do)

    def other_tail(k, c):
        lax.fori_loop(0, 2, lambda way, c: (tail(k, way, attend_other), c)[1], 0)

        @pl.when(jnp.logical_and(k + 2 - held == -1, jnp.logical_not(between)))
        def _():
            arrive(last)

        return c

    def fixed_tail(k, c):
        lax.fori_loop(0, 2, lambda way, c: (tail(k, way, attend_fixed), c)[1], 0)
        return c

    lax.fori_loop(0, held, other_tail, 0)

    slot = kv_head * (2 // Y) + (t if Y == 1 else 0)
    out_cols = pl.ds(pl.multiple_of(slot * width, width), width)

    def send_out(half, wait):
        for e in range(HH):
            i = half * HH + (h + e) % HH
            i_half, i_rows = part(i)
            send(obuf.at[i_half, i_rows, :], out_ref.at[:, out_cols],
                 out_send.at[half, e], out_recv, i, row_me, True, wait)

    for half in range(2):
        if half == 1:
            lax.fori_loop(0, held, fixed_tail, 0)
        outs = acc[half] * (1.0 / total[half])
        for g in range(HQ):
            o = jnp.transpose(outs[:, g * R:(g + 1) * R]).astype(jnp.bfloat16)
            obuf[half, :, g * HEAD_SIZE:(g + 1) * HEAD_SIZE] = o
        send_out(half, False)

    exchange_kv(True)
    exchange_q(True)

    def drain(row, c):
        pass_on(row, True)
        return c

    lax.fori_loop(0, B, drain, 0)
    for half in range(2):
        send_out(half, True)
    pltpu.make_async_copy(out_ref, out_ref, out_recv).wait()


def local(queries, keys, values, position, segment):
    H, B = lax.axis_size("head"), lax.axis_size("blk")
    T = queries.shape[1]
    Y = 2 * KV_HEADS // H
    HQ = QUERY_HEADS // H
    R = position.shape[1] // 2
    pairs = B * (2 * R) ** 2 * HQ * 17 // 32
    out = pl.pallas_call(
        functools.partial(kernel, H, B),
        out_shape=jax.ShapeDtypeStruct((T, QUERY_HEADS * HEAD_SIZE), jnp.bfloat16),
        in_specs=[pl.BlockSpec(memory_space=pltpu.HBM)] * 5,
        out_specs=pl.BlockSpec(memory_space=pl.ANY),
        scratch_shapes=[
            pltpu.VMEM((2, R, HQ * HEAD_SIZE), jnp.bfloat16),
            pltpu.VMEM((2, B, 2, R, HEAD_SIZE), jnp.bfloat16),
            pltpu.VMEM((B, 2, R, HEAD_SIZE), jnp.float32),
            pltpu.VMEM((2, R, HQ * HEAD_SIZE), jnp.bfloat16),
            pltpu.VMEM((2, 1, HQ * R), jnp.float32),
            pltpu.VMEM((2, 1, HQ * R), jnp.float32),
            pltpu.VMEM((2, HEAD_SIZE, HQ * R), jnp.float32),
            pltpu.VMEM((2, HEAD_SIZE, HQ * R), jnp.bfloat16),
            pltpu.SMEM(position.shape, jnp.int32),
            pltpu.VMEM(segment.shape, jnp.int32),
            pltpu.SemaphoreType.DMA((2,)),
            pltpu.SemaphoreType.DMA((2 + 2 // Y, KV_HEADS)),
            pltpu.SemaphoreType.DMA,
            pltpu.SemaphoreType.DMA((B,)),
            pltpu.SemaphoreType.DMA((B,)),
            pltpu.SemaphoreType.DMA((2, B)),
            pltpu.SemaphoreType.DMA((B,)),
            pltpu.SemaphoreType.DMA((2, H // 2)),
            pltpu.SemaphoreType.DMA,
        ],
        compiler_params=pltpu.CompilerParams(
            collective_id=0, has_side_effects=True, vmem_limit_bytes=60 * 2**20
        ),
        cost_estimate=pl.CostEstimate(
            flops=4 * pairs * HEAD_SIZE, bytes_accessed=8 * T * QUERY_HEADS * HEAD_SIZE, transcendentals=pairs
        ),
    )(queries[0], keys[0], values[0], position, segment)
    return out[None]


def solution(mesh):
    return jax.shard_map(
        local,
        mesh=mesh,
        in_specs=(P("blk", "head", None), P("blk", "head", None), P("blk", "head", None), P(), P()),
        out_specs=P("blk", "head", None),
        check_vma=False,
    )
```

```python
import functools
import math

import jax
import jax.numpy as jnp
from jax import lax
from jax.experimental import pallas as pl
from jax.experimental.pallas import tpu as pltpu
from jax.sharding import PartitionSpec as P

QUERY_HEADS = 16
KV_HEADS = 4
HEAD_SIZE = 128
MASKED = -1e30
SCALE = math.log2(math.e) / math.sqrt(HEAD_SIZE)
MESH = pl.DeviceIdType.MESH


def kernel(H, B, q_in, k_in, v_in, pos_ref, seg_ref, out_ref,
           qbuf, kv, segc, obuf, top, total, acc, qt, pos_buf, seg_buf, small,
           first_send, q_recv, row_recv, sib_recv, fwd_send, sib_send, out_send, out_recv):
    Y = 2 * KV_HEADS // H
    Z = B // Y
    HQ = QUERY_HEADS // H
    HH = H // 2
    T = q_in.shape[0]
    R = qbuf.shape[1]
    width = HQ * HEAD_SIZE
    h = lax.axis_index("head")
    b = lax.axis_index("blk")
    chip, t = h // 2, h % 2
    z, y = b // Y, b % Y
    kv_head = chip * Y + y
    sibling = chip * 2 + 1 - t
    row_me = z * Y + t % Y

    fetch = [pltpu.make_async_copy(pos_ref, pos_buf, small.at[0]), pltpu.make_async_copy(seg_ref, seg_buf, small.at[1])]
    for copy in fetch:
        copy.start()

    barrier = pltpu.get_barrier_semaphore()
    for i in range(H):
        for r in range(Y):
            @pl.when(jnp.logical_or(h != i, y != r))
            def _():
                pl.semaphore_signal(barrier, inc=1, device_id={"head": i, "blk": z * Y + r}, device_id_type=MESH)

    @pl.when(z > 0)
    def _():
        pl.semaphore_signal(barrier, inc=1, device_id={"head": h, "blk": b - Y}, device_id_type=MESH)

    @pl.when(z < Z - 1)
    def _():
        pl.semaphore_signal(barrier, inc=1, device_id={"head": h, "blk": b + Y}, device_id_type=MESH)

    near = (z > 0).astype(jnp.int32) + (z < Z - 1).astype(jnp.int32)
    pl.semaphore_wait(barrier, H * Y - 1 + near)

    def part(i):
        return i // HH, pl.ds(pl.multiple_of((i % HH) * T, T), T)

    my_half, my_rows = part(h)

    def send(src, dst, send_sem, recv_sem, head, blk, may_be_me, wait=False):
        def remote():
            copy = pltpu.make_async_remote_copy(
                src_ref=src, dst_ref=dst, send_sem=send_sem, recv_sem=recv_sem,
                device_id={"head": head, "blk": blk}, device_id_type=MESH)
            copy.wait_send() if wait else copy.start()

        if not may_be_me:
            remote()
            return
        other = jnp.logical_or(head != h, blk != b)
        pl.when(other)(remote)
        if not wait:
            @pl.when(jnp.logical_not(other))
            def _():
                pltpu.make_async_copy(src, dst, recv_sem).start()

    def exchange_kv(wait):
        for n, array in enumerate((k_in, v_in)):
            for d in range(KV_HEADS):
                d = (d + 1) % KV_HEADS
                k = (kv_head + d) % KV_HEADS
                cols = pl.ds(pl.multiple_of(k * HEAD_SIZE, HEAD_SIZE), HEAD_SIZE)
                send(array.at[:, cols], kv.at[n, b, my_half, my_rows, :],
                     first_send.at[n, d], row_recv.at[b],
                     (k // Y) * 2 + n, z * Y + k % Y, d == 0, wait)

    def exchange_q(wait):
        for half in range(2 // Y):
            for d in range(KV_HEADS):
                d = (d + 1) % KV_HEADS
                k = (kv_head + d) % KV_HEADS
                cols = pl.ds(pl.multiple_of((k * (2 // Y) + half) * width, width), width)
                core = half if Y == 1 else y
                send(q_in.at[:, cols], qbuf.at[my_half, my_rows, :],
                     first_send.at[2 + half, d], q_recv,
                     (k // Y) * 2 + core, z * Y + k % Y, d == 0, wait)

    def wait_row(row):
        pltpu.make_async_copy(kv.at[t, row], kv.at[t, row], row_recv.at[row]).wait()

    def wait_sibling(row):
        pltpu.make_async_copy(kv.at[1 - t, row], kv.at[1 - t, row], sib_recv.at[row]).wait()

    def pass_on(row, wait=False):
        def copy(head, blk, send_sem, recv_sem):
            c = pltpu.make_async_remote_copy(
                src_ref=kv.at[t, row], dst_ref=kv.at[t, row], send_sem=send_sem, recv_sem=recv_sem,
                device_id={"head": head, "blk": blk}, device_id_type=MESH)
            c.wait_send() if wait else c.start()

        j = row // Y

        @pl.when(jnp.logical_and(j <= z, z < Z - 1))
        def _():
            copy(h, b + Y, fwd_send.at[0, row], row_recv.at[row])

        @pl.when(jnp.logical_and(j >= z, z > 0))
        def _():
            copy(h, b - Y, fwd_send.at[1, row], row_recv.at[row])

        copy(sibling, b, sib_send.at[row], sib_recv.at[row])

    def seg_line(q_half):
        line = seg_buf[pl.ds(row_me, 1), :].astype(jnp.float32)
        return line[:, q_half * R:(q_half + 1) * R]

    def hide(col, line, extra=None):
        visible = jnp.concatenate([col] * (R // HEAD_SIZE), axis=1) == line
        if extra is not None:
            visible = jnp.logical_and(visible, extra)
        bias = jnp.where(visible, 0.0, MASKED)
        return jnp.concatenate([bias] * HQ, axis=1)

    def scores(keys, q_half):
        return jnp.dot(keys, qt[q_half], preferred_element_type=jnp.float32)

    def tile(s, bias, values_t):
        s = s + bias
        m = jnp.max(s, axis=0, keepdims=True)
        w = jnp.exp2((s - m) * SCALE)
        return (m, jnp.sum(w, axis=0, keepdims=True),
                jnp.dot(values_t, w.astype(jnp.bfloat16), preferred_element_type=jnp.float32))

    def merge(*states):
        m = functools.reduce(jnp.maximum, [x[0] for x in states])
        fades = [jnp.exp2((x[0] - m) * SCALE) for x in states]
        return (m, sum(x[1] * f for x, f in zip(states, fades)),
                sum(x[2] * f for x, f in zip(states, fades)))

    def load(which):
        return top[which], total[which], acc[which]

    def store(which, state):
        top[which], total[which], acc[which] = state

    def own():
        rows = lax.broadcasted_iota(jnp.int32, (R, R), 0)
        columns = lax.broadcasted_iota(jnp.int32, (R, R), 1)
        keys = [kv[0, row_me, half] for half in range(2)]
        values_t = [jnp.transpose(kv[1, row_me, half]) for half in range(2)]
        for half in range(2):
            for g in range(HQ):
                qt[half, :, g * R:(g + 1) * R] = jnp.transpose(qbuf[half, :, g * HEAD_SIZE:(g + 1) * HEAD_SIZE])
        s = [scores(keys[0], 0), scores(keys[1], 1), scores(keys[0], 1)]
        first = tile(s[0], hide(segc[row_me, 0], seg_line(0), rows <= columns), values_t[0])
        second = tile(s[1], hide(segc[row_me, 1], seg_line(1), rows <= columns), values_t[1])
        third = tile(s[2], hide(segc[row_me, 0], seg_line(1)), values_t[0])
        store(0, first)
        store(1, merge(second, third))

    def choose(row):
        which = (pos_buf[row, 0] > pos_buf[row_me, 0]).astype(jnp.int32)
        return which, which == 1

    def fixed_scores(row):
        return scores(kv[0, row, 0], 1)

    def fixed_tile(row, s):
        return tile(s, hide(segc[row, 0], seg_line(1)), jnp.transpose(kv[1, row, 0]))

    def other_scores(row):
        which, late = choose(row)
        return scores(jnp.where(late, kv[0, row, 1], kv[0, row, 0]), which)

    def other_tile(row, s):
        which, late = choose(row)
        col = jnp.where(late, segc[row, 1], segc[row, 0])
        m, tot, a = tile(s, hide(col, jnp.where(late, seg_line(1), seg_line(0))),
                         jnp.transpose(jnp.where(late, kv[1, row, 1], kv[1, row, 0])))
        return (jnp.where(late, MASKED, m), tot, a), (jnp.where(late, m, MASKED), tot, a)

    def attend(row):
        s_a, s_b = fixed_scores(row), other_scores(row)
        one = fixed_tile(row, s_a)
        to_early, to_later = other_tile(row, s_b)
        early = merge(load(0), to_early)
        later = merge(load(1), one, to_later)
        store(0, early)
        store(1, later)

    def attend_other(row):
        wait_sibling(row)
        to_early, to_later = other_tile(row, other_scores(row))
        early, later = merge(load(0), to_early), merge(load(1), to_later)
        store(0, early)
        store(1, later)

    def attend_fixed(row):
        store(1, merge(load(1), fixed_tile(row, fixed_scores(row))))

    def side(u, way, do):
        j = z + (1 + u // Y) * (2 * way - 1)

        @pl.when(jnp.logical_and(jnp.logical_and(j >= 0, j < Z), u >= 0))
        def _():
            do(j * Y + u % Y)

    def arrive_row(row):
        wait_row(row)
        pass_on(row)

    def use_row(row):
        wait_sibling(row)
        attend(row)

    def arrive(u):
        side(u, 0, arrive_row)
        side(u, 1, arrive_row)

    exchange_kv(False)
    exchange_q(False)
    for copy in fetch:
        copy.wait()
    for r in range(Y):
        wait_row(z * Y + r)
        pass_on(z * Y + r)

    def column(row, c):
        line = seg_buf[pl.ds(row, 1), :].astype(jnp.float32)
        segc[row] = jnp.transpose(jnp.broadcast_to(line, (HEAD_SIZE, 2 * R))).reshape(2, R, HEAD_SIZE)
        return c

    lax.fori_loop(0, B, column, 0)

    units = (Z - 1) * Y
    between = jnp.logical_and(z > 0, z < Z - 1)
    ahead = jnp.where(between, 4, 2)
    for u in range(min(2, units)):
        arrive(u)
    pltpu.make_async_copy(qbuf, qbuf, q_recv).wait()
    for r in range(Y):
        wait_sibling(z * Y + r)
    own()

    def early(u):
        @pl.when(jnp.logical_and(between, u < units))
        def _():
            arrive(u)

    early(2)
    for r in range(1, Y):
        attend(z * Y + (t + r) % Y)
    early(3)

    def step(u, c):
        def each(way, c):
            side(u, way, use_row)
            return c

        lax.fori_loop(0, 2, each, 0)

        @pl.when(u + ahead < units)
        def _():
            arrive(u + ahead)

        return c

    last = jnp.maximum(z, Z - 1 - z) * Y - 1
    held = jnp.where(between, 3, 1)
    lax.fori_loop(0, jnp.maximum(last + 1 - held, 0), step, 0)

    def tail(k, way, do):
        side(last + 1 - held + k, way, do)

    def other_tail(k, c):
        lax.fori_loop(0, 2, lambda way, c: (tail(k, way, attend_other), c)[1], 0)

        @pl.when(jnp.logical_and(k + 2 - held == -1, jnp.logical_not(between)))
        def _():
            arrive(last)

        return c

    def fixed_tail(k, c):
        lax.fori_loop(0, 2, lambda way, c: (tail(k, way, attend_fixed), c)[1], 0)
        return c

    lax.fori_loop(0, held, other_tail, 0)

    slot = kv_head * (2 // Y) + (t if Y == 1 else 0)
    out_cols = pl.ds(pl.multiple_of(slot * width, width), width)

    def send_out(half, wait):
        for e in range(HH):
            i = half * HH + (h + e) % HH
            i_half, i_rows = part(i)
            send(obuf.at[i_half, i_rows, :], out_ref.at[:, out_cols],
                 out_send.at[half, e], out_recv, i, row_me, True, wait)

    for half in range(2):
        if half == 1:
            lax.fori_loop(0, held, fixed_tail, 0)
        outs = acc[half] * (1.0 / total[half])
        for g in range(HQ):
            o = jnp.transpose(outs[:, g * R:(g + 1) * R]).astype(jnp.bfloat16)
            obuf[half, :, g * HEAD_SIZE:(g + 1) * HEAD_SIZE] = o
        send_out(half, False)

    exchange_kv(True)
    exchange_q(True)

    def drain(row, c):
        pass_on(row, True)
        return c

    lax.fori_loop(0, B, drain, 0)
    for half in range(2):
        send_out(half, True)
    pltpu.make_async_copy(out_ref, out_ref, out_recv).wait()


def local(queries, keys, values, position, segment):
    H, B = lax.axis_size("head"), lax.axis_size("blk")
    T = queries.shape[1]
    Y = 2 * KV_HEADS // H
    HQ = QUERY_HEADS // H
    R = position.shape[1] // 2
    pairs = B * (2 * R) ** 2 * HQ * 17 // 32
    out = pl.pallas_call(
        functools.partial(kernel, H, B),
        out_shape=jax.ShapeDtypeStruct((T, QUERY_HEADS * HEAD_SIZE), jnp.bfloat16),
        in_specs=[pl.BlockSpec(memory_space=pltpu.HBM)] * 5,
        out_specs=pl.BlockSpec(memory_space=pl.ANY),
        scratch_shapes=[
            pltpu.VMEM((2, R, HQ * HEAD_SIZE), jnp.bfloat16),
            pltpu.VMEM((2, B, 2, R, HEAD_SIZE), jnp.bfloat16),
            pltpu.VMEM((B, 2, R, HEAD_SIZE), jnp.float32),
            pltpu.VMEM((2, R, HQ * HEAD_SIZE), jnp.bfloat16),
            pltpu.VMEM((2, 1, HQ * R), jnp.float32),
            pltpu.VMEM((2, 1, HQ * R), jnp.float32),
            pltpu.VMEM((2, HEAD_SIZE, HQ * R), jnp.float32),
            pltpu.VMEM((2, HEAD_SIZE, HQ * R), jnp.bfloat16),
            pltpu.SMEM(position.shape, jnp.int32),
            pltpu.VMEM(segment.shape, jnp.int32),
            pltpu.SemaphoreType.DMA((2,)),
            pltpu.SemaphoreType.DMA((2 + 2 // Y, KV_HEADS)),
            pltpu.SemaphoreType.DMA,
            pltpu.SemaphoreType.DMA((B,)),
            pltpu.SemaphoreType.DMA((B,)),
            pltpu.SemaphoreType.DMA((2, B)),
            pltpu.SemaphoreType.DMA((B,)),
            pltpu.SemaphoreType.DMA((2, H // 2)),
            pltpu.SemaphoreType.DMA,
        ],
        compiler_params=pltpu.CompilerParams(
            collective_id=0, has_side_effects=True, vmem_limit_bytes=60 * 2**20
        ),
        cost_estimate=pl.CostEstimate(
            flops=4 * pairs * HEAD_SIZE, bytes_accessed=8 * T * QUERY_HEADS * HEAD_SIZE, transcendentals=pairs
        ),
    )(queries[0], keys[0], values[0], position, segment)
    return out[None]


def solution(mesh):
    return jax.shard_map(
        local,
        mesh=mesh,
        in_specs=(P("blk", "head", None), P("blk", "head", None), P("blk", "head", None), P(), P()),
        out_specs=P("blk", "head", None),
        check_vma=False,
    )
```
